32 devices in a mesh: space: 4 (over x, core), snap: 8 (over z, y).
Axes of the slice: x: 2, y: 2, z: 4, core: 2. Of those that a mesh axis runs over, the one named last changes fastest.
Arguments:
- velocity: bfloat16 [64, 3, 8, 32, 128], P('snap', None, 'space'), may hold values from -40 to 40
- block_id: int32 [8, 32, 128], P('space'), may hold values from 0 to 7
- metric: float32 [8, 3], replicated, may hold values from 0.5 to 2
- leaf_rot: float32 [8, 8, 16], P('snap'), may hold values from -2 to 2
- merge_rot: float32 [7, 32, 16], replicated, may hold values from -1 to 1
- merge_order: int32 [7], replicated, may hold values from 0 to 1
- ref_cell: int32 [16], replicated, may hold values from 0 to 98303
Outputs:
- modes: float32 [16, 3, 8, 4096], P(None, None, 'space', 'snap')
The draws below stay inside these ranges and needn't reach their ends.
All inputs are finite; a program needn't handle non-finite values.
Results may differ from the reference program's by a relative error of at most 0.0003.
Values may be sent and summed in bfloat16 or wider, within the bound.
A program may use at most 64 MiB of HBM per device.

```python
import math
import jax
import jax.numpy as jnp
from jax import lax

S = 8
NX = 32
NZ = 128
R = 16
NBLK = 8
SNAPS = 64
NY = 8
LEVELS = 3
NODES = 7
N_SNAP = 8


def draw_velocity(key, part):
    key_base = jax.random.fold_in(key, 11)
    key_cells = jax.random.fold_in(key, 12)
    shape = (SNAPS, 3, NY, NX, NZ)
    wall_pos = (jnp.arange(NY, dtype=jnp.float32) + 0.5) / NY
    profile = (1.0 + 2.0 * wall_pos).reshape(1, 1, NY, 1, 1)
    cell_scale = 0.3 * 10.0 ** jax.random.uniform(key_cells, (1, 3, NY, NX, NZ), jnp.float32)
    base = jnp.clip(jax.random.normal(key_base, shape, jnp.float32), -4.0, 4.0)
    field = base * cell_scale * profile
    return field.astype(jnp.bfloat16)


def set_ends(values, key, least, top_value):
    longest = values.shape.index(max(values.shape))
    spots = []
    for shift in (0, 1):
        where = [jax.random.randint(jax.random.fold_in(key, axis), (), 0, length) for axis, length in enumerate(values.shape)]
        where[longest] = (where[longest] + shift) % values.shape[longest]
        spots.append(tuple(where))
    return values.at[spots[0]].set(least).at[spots[1]].set(top_value)


def shard_levels(rng, dims, split, low, high):
    def one(axis_at, blocks):
        steps = jax.random.uniform(jax.random.fold_in(jax.random.fold_in(rng, 6), axis_at), (blocks,), jnp.float32, low / len(split), high / len(split))
        return jnp.repeat(jnp.exp(steps), dims[axis_at] // blocks).reshape((-1,) + (1,) * (len(dims) - axis_at - 1))

    level = one(*split[0])
    for cut in split[1:]:
        level = level * one(*cut)
    return level


def centred(stream_key, shape, deviation, limit, pieces=(), kind=jnp.bfloat16):
    result = deviation * jax.random.normal(stream_key, shape, jnp.float32)
    if pieces:
        result = result * shard_levels(stream_key, shape, pieces, -0.22, 0.18)
    return jnp.clip(result, -limit, limit).astype(kind)


def setup_inputs(seed: int = 0) -> dict:
    splits = jax.random.split(jax.random.key(seed), 8)
    velocity = draw_velocity(jax.random.fold_in(splits[7], 71), 0)
    block_id = set_ends(jax.random.randint(splits[1], (NY, NX, NZ), 0, NBLK), jax.random.fold_in(splits[1], 1), 0, NBLK - 1).astype(jnp.int32)
    metric = jnp.clip(jnp.exp(jax.random.uniform(splits[2], (NBLK, 3), jnp.float32, math.log(0.5), math.log(2.0))), 0.5, 2.0)
    leaf_rot = centred(splits[3], (N_SNAP, S, R), S ** -0.5, 2.0, ((0, 8),), jnp.float32)
    merge_rot = centred(splits[4], (NODES, 2 * R, R), (2 * R) ** -0.5, 1.0, (), jnp.float32)
    merge_order = set_ends(jax.random.randint(splits[5], (NODES,), 0, 2), jax.random.fold_in(splits[5], 1), 0, 1).astype(jnp.int32)
    ref_cell = set_ends(jax.random.randint(splits[6], (R,), 0, 3 * NY * NX * NZ), jax.random.fold_in(splits[6], 1), 0, (3 * NY * NX * NZ) - 1).astype(jnp.int32)
    return {"velocity": velocity, "block_id": block_id, "metric": metric, "leaf_rot": leaf_rot, "merge_rot": merge_rot, "merge_order": merge_order, "ref_cell": ref_cell}


HIGHEST = lax.Precision.HIGHEST

def along_x(field, spacing):
    return spacing[0] * (jnp.roll(field, -1, axis=2) - jnp.roll(field, 1, axis=2)) * 0.5

def along_z(field, spacing):
    return spacing[2] * (jnp.roll(field, -1, axis=3) - jnp.roll(field, 1, axis=3)) * 0.5

def along_y(field, spacing):
    padded = jnp.pad(field, ((0, 0), (1, 1), (0, 0), (0, 0)))
    return spacing[1] * (padded[:, 2:] - padded[:, :-2]) * 0.5

def vorticity_of(vel_block, spacing):
    vel_u = vel_block[:, 0]
    vel_v = vel_block[:, 1]
    vel_w = vel_block[:, 2]
    omega_x = along_y(vel_w, spacing) - along_z(vel_v, spacing)
    omega_y = along_z(vel_u, spacing) - along_x(vel_w, spacing)
    omega_z = along_x(vel_v, spacing) - along_y(vel_u, spacing)
    return jnp.stack([omega_x, omega_y, omega_z], axis=1)

def reference(velocity, block_id, metric, leaf_rot, merge_rot, merge_order, ref_cell):
    spacing = jnp.moveaxis(metric[block_id], -1, 0)
    rank = leaf_rot.shape[2]

    def leaf_block(group):
        vel_block = velocity[group * S:(group + 1) * S].astype(jnp.float32)
        omega = vorticity_of(vel_block, spacing).reshape(S, -1)
        return jnp.dot(leaf_rot[group].T, omega, precision=HIGHEST, preferred_element_type=jnp.float32)

    def node_block(tree_level, node_k):
        if tree_level < 0:
            return leaf_block(node_k)
        left_child = node_block(tree_level - 1, 2 * node_k)
        right_child = node_block(tree_level - 1, 2 * node_k + 1)
        node_id = N_SNAP - (N_SNAP >> tree_level) + node_k
        rotation = merge_rot[node_id]
        order_bit = merge_order[node_id]
        first = jnp.where(order_bit == 0, left_child, right_child)
        second = jnp.where(order_bit == 0, right_child, left_child)
        merged = jnp.dot(rotation[:rank].T, first, precision=HIGHEST, preferred_element_type=jnp.float32)
        merged = merged + jnp.dot(rotation[rank:].T, second, precision=HIGHEST, preferred_element_type=jnp.float32)
        gram_total = jnp.dot(merged, merged.T, precision=HIGHEST, preferred_element_type=jnp.float32)
        scale = (jnp.trace(gram_total) + 1e-06) / rank
        factor = 1.5 * jnp.eye(rank, dtype=jnp.float32) - 0.5 * gram_total / scale
        return jnp.dot(factor.T, merged, precision=HIGHEST, preferred_element_type=jnp.float32)
    root = node_block(LEVELS - 1, 0)
    norm_sq = lax.optimization_barrier(jnp.sum(root * root, axis=1))
    floor_value = 0.5 * jnp.sqrt(norm_sq / (3 * NY * NX * NZ) + 1e-06)
    value = jnp.take_along_axis(root, ref_cell.astype(jnp.int32)[:, None], axis=1)[:, 0]
    sign = value / jnp.maximum(jnp.abs(value), floor_value)
    modes = root * sign[:, None]
    return modes.reshape(rank, 3, NY, NX * NZ)
```

```python
import functools

import jax
import jax.numpy as jnp
from jax import lax
from jax.experimental import pallas as pl
from jax.experimental.pallas import tpu as pltpu
from jax.sharding import PartitionSpec as P

HIGHEST = lax.Precision.HIGHEST
MESH = pl.DeviceIdType.MESH
F32 = jnp.float32
BF16 = jnp.bfloat16


def exact(left, right, dims=((1,), (0,))):
    return lax.dot_general(left, right, (dims, ((), ())), precision=HIGHEST, preferred_element_type=F32)


def product(left, right, dims=((1,), (0,))):
    return lax.dot_general(left, right, (dims, ((), ())), preferred_element_type=F32)


def iota(shape, dim):
    return lax.broadcasted_iota(jnp.int32, shape, dim)


def ortho_factor(gram, rank):
    size = gram.shape[0]
    eye = iota(gram.shape, 0) == iota(gram.shape, 1)
    same = iota(gram.shape, 0) // rank == iota(gram.shape, 1) // rank
    diagonal = jnp.sum(jnp.where(eye, gram, 0.0), axis=0, keepdims=True)
    if size > rank:
        spread = jnp.broadcast_to(diagonal, (8, size))
        trace = exact(spread, same.astype(F32))[:1]
    else:
        trace = jnp.sum(diagonal, axis=1, keepdims=True)
    scale = (trace + 1e-06) / rank
    return 1.5 * eye.astype(F32) - jnp.where(same, 0.5 * gram / scale, 0.0)


def kernel(
    dims,
    vel_ref, block_ref, metric_ref, leaf_ref, rot_ref, order_ref, cell_ref, out_ref,
    velf, send_u, send_vw, recv_u, recv_vw, stage, halo, lead, spacing, parts_hi, parts_lo,
    gram_own, gram_space, gram_snap, gram_all,
    sem_u_s, sem_u_r, sem_vw_s, sem_vw_r, sem_lead_s, sem_lead_r, sem_halo_s, sem_halo_r,
    sem_a_s, sem_a_r, sem_b_s, sem_b_r, sem_c_s, sem_c_r,
):
    groups, spaces = dims
    here, _, rows_y, cells_x, cells_z = vel_ref.shape
    rank = leaf_ref.shape[2]
    blocks = metric_ref.shape[0]
    total = groups * here
    width_x = cells_x // groups
    me = lax.axis_index("snap")
    sp = lax.axis_index("space")
    first_x = me * width_x

    def peer(step):
        return lax.rem(me + step, groups)

    def mate(step):
        return lax.rem(sp + step, spaces)

    barrier = pltpu.get_barrier_semaphore()
    for step in range(1, spaces):
        pl.semaphore_signal(barrier, inc=1, device_id={"space": mate(step)}, device_id_type=MESH)

    def greet(step, carry):
        pl.semaphore_signal(barrier, inc=1, device_id={"snap": peer(step)}, device_id_type=MESH)
        return carry

    lax.fori_loop(1, groups, greet, 0)

    stretch = 3 * rows_y * cells_x

    def widen(snap, carry):
        start = pl.multiple_of(snap * stretch, stretch)
        velf[pl.ds(start, stretch), :] = vel_ref[snap].reshape(stretch, cells_z).astype(F32)
        return carry

    lax.fori_loop(0, here, widen, 0)

    def tile(comp, x):
        pieces = [
            velf[pl.ds((comp * rows_y + y) * cells_x + x, here, stride=stretch), :]
            for y in range(rows_y)
        ]
        return jnp.concatenate(pieces, axis=0).astype(BF16)

    def regroup(x, carry):
        send_u[x] = tile(0, x)
        send_vw[0, x + 1] = tile(1, x)
        send_vw[1, x + 1] = tile(2, x)
        return carry

    lax.fori_loop(0, cells_x, regroup, 0, unroll=4)
    for comp in range(2):
        send_vw[comp, 0] = send_vw[comp, cells_x]
        send_vw[comp, cells_x + 1] = send_vw[comp, 1]

    lead_width = lead.shape[2]
    turn = rot_ref[me // 2]
    pick = (order_ref[me // 2] - me % 2).astype(F32)
    pick = pick * pick
    turn_own = turn[:rank] * (1.0 - pick) + turn[rank:] * pick
    lead_own = exact(leaf_ref[0], turn_own)
    repeat = (iota((rank, lead_width), 1) % rank == iota((rank, lead_width), 0)).astype(F32)
    lead_wide = exact(lead_own, repeat)
    lead[me] = jnp.where(iota(lead_wide.shape, 1) // rank == me // 2, lead_wide, 0.0)

    pl.semaphore_wait(barrier, groups + spaces - 2)

    def copies(step):
        to = peer(step)
        start = to * width_x
        return (
            pltpu.make_async_remote_copy(
                send_vw.at[:, pl.ds(start, width_x + 2)], recv_vw.at[me],
                sem_vw_s.at[step], sem_vw_r.at[me], device_id={"snap": to}, device_id_type=MESH,
            ),
            pltpu.make_async_remote_copy(
                send_u.at[pl.ds(start, width_x)], recv_u.at[me],
                sem_u_s.at[step], sem_u_r.at[me], device_id={"snap": to}, device_id_type=MESH,
            ),
            pltpu.make_async_remote_copy(
                lead.at[me], lead.at[me],
                sem_lead_s.at[step], sem_lead_r.at[me], device_id={"snap": to}, device_id_type=MESH,
            ),
        )

    def arrivals(source):
        return (
            pltpu.make_async_remote_copy(
                recv_vw.at[source], recv_vw.at[source],
                sem_vw_s.at[0], sem_vw_r.at[source], device_id={"snap": source}, device_id_type=MESH,
            ),
            pltpu.make_async_remote_copy(
                recv_u.at[source], recv_u.at[source],
                sem_u_s.at[0], sem_u_r.at[source], device_id={"snap": source}, device_id_type=MESH,
            ),
            pltpu.make_async_remote_copy(
                lead.at[source], lead.at[source],
                sem_lead_s.at[0], sem_lead_r.at[source], device_id={"snap": source}, device_id_type=MESH,
            ),
        )

    def launch(step, carry):
        for copy in copies(step):
            copy.start()
        return carry

    lax.fori_loop(1, groups, launch, 0)

    def halo_copy(side, group):
        to = sp + 1 if side == 0 else sp - 1
        return pltpu.make_async_remote_copy(
            stage.at[side, group], halo.at[side, group],
            sem_halo_s.at[side, group], sem_halo_r.at[side, group],
            device_id={"space": to}, device_id_type=MESH,
        )

    def forward(group):
        for x in range(width_x):
            u_here = recv_u[group, x].astype(F32)
            w_here = recv_vw[group, 1, x + 1].astype(F32)
            stage[1, group, x] = jnp.concatenate([u_here[:here], w_here[:here]], axis=0).astype(BF16)
            stage[0, group, x] = jnp.concatenate([u_here[-here:], w_here[-here:]], axis=0).astype(BF16)

        @pl.when(sp < spaces - 1)
        def _():
            halo_copy(0, group).start()

        @pl.when(sp > 0)
        def _():
            halo_copy(1, group).start()

    recv_u[me] = send_u[pl.ds(first_x, width_x)]
    recv_vw[me] = send_vw[:, pl.ds(first_x, width_x + 2)]
    forward(me)

    @pl.when(sp == 0)
    def _():
        halo[0] = jnp.zeros(halo.shape[1:], BF16)

    @pl.when(sp == spaces - 1)
    def _():
        halo[1] = jnp.zeros(halo.shape[1:], BF16)

    for y in range(rows_y):
        for x in range(width_x):
            ids = block_ref[y, pl.ds(first_x + x, 1), :]
            for axis in range(3):
                value = jnp.zeros((1, cells_z), F32)
                for block in range(blocks):
                    value = jnp.where(ids == block, metric_ref[block, axis], value)
                spacing[axis, y, pl.ds(x, 1), :] = 0.5 * value

    plane = cells_x * cells_z
    parts_hi[pl.ds(total, parts_hi.shape[0] - total), :] = jnp.zeros(
        (parts_hi.shape[0] - total, parts_hi.shape[1]), BF16
    )
    parts_lo[pl.ds(total, parts_lo.shape[0] - total), :] = jnp.zeros(
        (parts_lo.shape[0] - total, parts_lo.shape[1]), BF16
    )
    row = iota((rank, cells_z), 0)
    wanted = jnp.zeros((rank, cells_z), jnp.int32)
    for mode in range(rank):
        wanted = jnp.where(row == mode, cell_ref[mode], wanted)
    for comp in range(3):
        for y in range(rows_y):
            for x in range(width_x):
                base = ((comp * rows_y * spaces + sp * rows_y + y) * cells_x + first_x + x) * cells_z
                hit = jnp.where(wanted == base + iota((rank, cells_z), 1), 1.0, 0.0)
                column = ((comp * rows_y + y) * width_x + x) * cells_z
                parts_hi[pl.ds(total, rank), pl.ds(column, cells_z)] = hit.astype(BF16)

    depth = groups.bit_length() - 1
    turns = []
    for level in range(1, depth):
        nodes = groups >> level + 1
        stacked = []
        for k in range(nodes):
            node = groups - (groups >> level) + k
            plain = rot_ref[node]
            swapped = jnp.concatenate([plain[rank:], plain[:rank]], axis=0)
            flag = order_ref[node].astype(F32)
            stacked.append(plain * (1.0 - flag) + swapped * flag)
        stacked = stacked[0] if nodes == 1 else jnp.concatenate(stacked, axis=0)
        if nodes > 1:
            shape = (rank, rank * nodes)
            copy_out = (iota(shape, 1) % rank == iota(shape, 0)).astype(F32)
            stacked = exact(stacked, copy_out)
            stacked = jnp.where(
                iota(stacked.shape, 0) // (2 * rank) == iota(stacked.shape, 1) // rank, stacked, 0.0
            )
        turns.append(stacked)

    def receive(step, carry):
        source = lax.rem(me - step + groups, groups)
        for copy in arrivals(source):
            copy.wait_recv()
        forward(source)
        return carry

    lax.fori_loop(1, groups, receive, 0)

    def split_store(start, column, value):
        high = value.astype(BF16)
        low = (value - high.astype(F32)).astype(BF16)
        parts_hi[pl.ds(start, 2 * here), pl.ds(column, cells_z)] = high
        parts_lo[pl.ds(start, 2 * here), pl.ds(column, cells_z)] = low

    def wait_halo(group):
        @pl.when(sp > 0)
        def _():
            halo_copy(0, group).wait_recv()

        @pl.when(sp < spaces - 1)
        def _():
            halo_copy(1, group).wait_recv()

    def curl(pair, carry):
        pair_groups = (2 * pair, 2 * pair + 1)
        start = pl.multiple_of(pair * 2 * here, 2 * here)
        for group in pair_groups:
            wait_halo(group)

        def load(ref, *index):
            both = [ref[(group, *index)].astype(F32) for group in pair_groups]
            return [
                jnp.concatenate([item[y * here:(y + 1) * here] for item in both], axis=0)
                for y in range(rows_y)
            ]

        def load_halo(side, x):
            both = [halo[side, group, x].astype(F32) for group in pair_groups]
            return [jnp.concatenate([item[c * here:(c + 1) * here] for item in both], axis=0) for c in range(2)]

        def along_z(field):
            return pltpu.roll(field, cells_z - 1, 1) - pltpu.roll(field, 1, 1)

        for x in range(width_x):
            u_at = load(recv_u, x)
            v_at = load(recv_vw, 0, x + 1)
            w_at = load(recv_vw, 1, x + 1)
            v_ends = load(recv_vw, 0, x), load(recv_vw, 0, x + 2)
            w_ends = load(recv_vw, 1, x), load(recv_vw, 1, x + 2)
            below = load_halo(0, x)
            above = load_halo(1, x)
            for y in range(rows_y):
                hx, hy, hz = (spacing[axis, y, pl.ds(x, 1), :] for axis in range(3))
                u_down = u_at[y - 1] if y > 0 else below[0]
                w_down = w_at[y - 1] if y > 0 else below[1]
                u_up = u_at[y + 1] if y < rows_y - 1 else above[0]
                w_up = w_at[y + 1] if y < rows_y - 1 else above[1]
                omega = (
                    hy * (w_up - w_down) - hz * along_z(v_at[y]),
                    hz * along_z(u_at[y]) - hx * (w_ends[1][y] - w_ends[0][y]),
                    hx * (v_ends[1][y] - v_ends[0][y]) - hy * (u_up - u_down),
                )
                for comp in range(3):
                    split_store(start, ((comp * rows_y + y) * width_x + x) * cells_z, omega[comp])
        return carry

    lax.fori_loop(0, groups // 2, curl, 0)

    high = parts_hi[:total]
    low = parts_lo[:total]
    last = ((1,), (1,))
    gram_own[...] = (
        product(high, parts_hi[...], last) + product(low, parts_hi[...], last) + product(high, parts_lo[...], last)
    ).reshape(gram_own.shape)

    def copy_a(step):
        to = mate(step)
        return pltpu.make_async_remote_copy(
            gram_own.at[to], gram_space.at[step], sem_a_s.at[step], sem_a_r.at[step],
            device_id={"space": to}, device_id_type=MESH,
        )

    for step in range(1, spaces):
        copy_a(step).start()
    lead_all = lead[...].reshape(total, lead_width)[:, :rank * groups // 2]
    part = gram_own[sp]
    for step in range(1, spaces):
        copy_a(step).wait_recv()
        part = part + gram_space[step]
    gram_snap[0] = part

    def copy_b(step):
        return pltpu.make_async_remote_copy(
            gram_snap.at[0], gram_snap.at[step], sem_b_s.at[step], sem_b_r.at[step],
            device_id={"snap": peer(step)}, device_id_type=MESH,
        )

    def start_b(step, carry):
        copy_b(step).start()
        return carry

    def finish_b(step, carry):
        copy_b(step).wait_recv()
        return carry + gram_snap[step]

    lax.fori_loop(1, groups, start_b, 0)
    gram_all[sp] = lax.fori_loop(1, groups, finish_b, part)

    def copy_c(step, owner):
        return pltpu.make_async_remote_copy(
            gram_all.at[owner], gram_all.at[owner], sem_c_s.at[step], sem_c_r.at[step],
            device_id={"space": mate(step)}, device_id_type=MESH,
        )

    for step in range(1, spaces):
        copy_c(step, sp).start()
    for step in range(1, spaces):
        copy_c(step, lax.rem(sp - step + spaces, spaces)).wait_recv()
    summed = gram_all[...].reshape(total, gram_all.shape[2])

    first = ((0,), (0,))
    entries = summed[:, total:total + rank]
    maps = lead_all
    gram = exact(maps, exact(summed[:, :total], maps), first)
    for turn in turns:
        step_map = exact(ortho_factor(gram, rank), turn)
        gram = exact(step_map, exact(gram, step_map), first)
        maps = exact(maps, step_map)
    factor = ortho_factor(gram, rank)
    value = jnp.sum(factor * exact(maps, entries, first), axis=0, keepdims=True)
    norm_sq = jnp.sum(factor * exact(gram, factor), axis=0, keepdims=True)
    cells_all = 3 * rows_y * spaces * plane
    floor = 0.5 * jnp.sqrt(norm_sq / cells_all + 1e-06)
    sign = value / jnp.maximum(jnp.abs(value), floor)
    mix = exact(factor * sign, maps, ((0,), (1,)))
    mix_high = mix.astype(BF16)
    mix_low = (mix - mix_high.astype(F32)).astype(BF16)
    both = product(jnp.concatenate([mix_high, mix_low], axis=0), high)
    out_ref[...] = both[:rank] + both[rank:] + product(mix_high, low)

    def finish(step, carry):
        for copy in copies(step):
            copy.wait_send()
        copy_b(step).wait_send()
        return carry

    lax.fori_loop(1, groups, finish, 0)
    for step in range(1, spaces):
        copy_a(step).wait_send()
        copy_c(step, sp).wait_send()

    def finish_halo(group, carry):
        @pl.when(sp < spaces - 1)
        def _():
            halo_copy(0, group).wait_send()

        @pl.when(sp > 0)
        def _():
            halo_copy(1, group).wait_send()

        return carry

    lax.fori_loop(0, groups, finish_halo, 0)


def padded(size, unit):
    return -(-size // unit) * unit


def local(velocity, block_id, metric, leaf_rot, merge_rot, merge_order, ref_cell):
    here, _, rows_y, cells_x, cells_z = velocity.shape
    rank = leaf_rot.shape[2]
    groups = lax.axis_size("snap")
    spaces = lax.axis_size("space")
    total = groups * here
    width_x = cells_x // groups
    tile_rows = rows_y * here
    cells = 3 * rows_y * width_x * cells_z
    gram_width = padded(total + rank, 128)
    share = total // spaces
    lead_width = padded(rank * groups // 2, 128)
    vmem = pl.BlockSpec(memory_space=pltpu.VMEM)
    smem = pl.BlockSpec(memory_space=pltpu.SMEM)
    dma = pltpu.SemaphoreType.DMA
    modes = pl.pallas_call(
        functools.partial(kernel, (groups, spaces)),
        out_shape=jax.ShapeDtypeStruct((rank, cells), F32),
        in_specs=[vmem, vmem, smem, vmem, vmem, smem, smem],
        out_specs=vmem,
        scratch_shapes=[
            pltpu.VMEM((here * 3 * rows_y * cells_x, cells_z), F32),
            pltpu.VMEM((cells_x, tile_rows, cells_z), BF16),
            pltpu.VMEM((2, cells_x + 2, tile_rows, cells_z), BF16),
            pltpu.VMEM((groups, width_x, tile_rows, cells_z), BF16),
            pltpu.VMEM((groups, 2, width_x + 2, tile_rows, cells_z), BF16),
            pltpu.VMEM((2, groups, width_x, 2 * here, cells_z), BF16),
            pltpu.VMEM((2, groups, width_x, 2 * here, cells_z), BF16),
            pltpu.VMEM((groups, here, lead_width), F32),
            pltpu.VMEM((3, rows_y, width_x, cells_z), F32),
            pltpu.VMEM((gram_width, cells), BF16),
            pltpu.VMEM((gram_width, cells), BF16),
            pltpu.VMEM((spaces, share, gram_width), F32),
            pltpu.VMEM((spaces, share, gram_width), F32),
            pltpu.VMEM((groups, share, gram_width), F32),
            pltpu.VMEM((spaces, share, gram_width), F32),
        ]
        + [dma((groups,))] * 6
        + [dma((2, groups))] * 2
        + [dma((spaces,))] * 2
        + [dma((groups,))] * 2
        + [dma((spaces,))] * 2,
        compiler_params=pltpu.CompilerParams(
            collective_id=0, has_side_effects=True, vmem_limit_bytes=32 * 1024 * 1024
        ),
    )(velocity, block_id, metric, leaf_rot, merge_rot, merge_order, ref_cell)
    return modes.reshape(rank, 3, rows_y, width_x * cells_z)


def solution(mesh):
    placed = (
        P("snap", None, "space", None, None),
        P("space", None, None),
        P(),
        P("snap", None, None),
        P(),
        P(),
        P(),
    )
    return jax.shard_map(
        local, mesh=mesh, in_specs=placed, out_specs=P(None, None, "space", "snap"), check_vma=False
    )
```

```python
import functools

import jax
import jax.numpy as jnp
from jax import lax
from jax.experimental import pallas as pl
from jax.experimental.pallas import tpu as pltpu
from jax.sharding import PartitionSpec as P

HIGHEST = lax.Precision.HIGHEST
MESH = pl.DeviceIdType.MESH
F32 = jnp.float32
BF16 = jnp.bfloat16


def exact(left, right, dims=((1,), (0,))):
    return lax.dot_general(left, right, (dims, ((), ())), precision=HIGHEST, preferred_element_type=F32)


def product(left, right, dims=((1,), (0,))):
    return lax.dot_general(left, right, (dims, ((), ())), preferred_element_type=F32)


def split(value):
    high = value.astype(BF16)
    return high, (value - high.astype(F32)).astype(BF16)


def close(left, right, dims=((1,), (0,))):
    left_high, left_low = split(left)
    right_high, right_low = split(right)
    return (
        product(left_high, right_high, dims)
        + product(left_high, right_low, dims)
        + product(left_low, right_high, dims)
    )


def iota(shape, dim):
    return lax.broadcasted_iota(jnp.int32, shape, dim)


def ortho_factor(gram, rank):
    size = gram.shape[0]
    eye = iota(gram.shape, 0) == iota(gram.shape, 1)
    same = iota(gram.shape, 0) // rank == iota(gram.shape, 1) // rank
    diagonal = jnp.sum(jnp.where(eye, gram, 0.0), axis=0, keepdims=True)
    node_of = iota((1, size), 1) // rank
    trace = jnp.zeros((1, size), F32)
    for node in range(size // rank):
        own = jnp.where(node_of == node, diagonal, 0.0)
        trace = jnp.where(node_of == node, jnp.sum(own, axis=1, keepdims=True), trace)
    scale = (trace + 1e-06) / rank
    return 1.5 * eye.astype(F32) - jnp.where(same, 0.5 * gram / scale, 0.0)


def kernel(
    dims,
    vel_hbm, block_ref, metric_ref, leaf_ref, rot_ref, order_ref, cell_ref, out_ref,
    vel_ref, velf, send_u, send_vw, recv_u, recv_vw, stage, halo, lead, spacing, parts,
    gram_own, gram_space, gram_snap, gram_all,
    sem_vel, sem_u_s, sem_u_r, sem_vw_s, sem_vw_r, sem_lead_s, sem_lead_r, sem_halo_s, sem_halo_r,
    sem_a_s, sem_a_r, sem_b_s, sem_b_r, sem_c_s, sem_c_r,
):
    groups, spaces = dims
    here, _, rows_y, cells_x, cells_z = vel_ref.shape
    rank = leaf_ref.shape[2]
    blocks = metric_ref.shape[1]
    total = groups * here
    width_x = cells_x // groups
    me = lax.axis_index("snap")
    sp = lax.axis_index("space")
    first_x = me * width_x

    half = groups // 2
    load_velocity = pltpu.make_async_copy(vel_hbm, vel_ref, sem_vel)
    load_velocity.start()

    def peer(step):
        return lax.rem(me + step, groups)

    def mate(step):
        return lax.rem(sp + step, spaces)

    barrier = pltpu.get_barrier_semaphore()
    for step in range(1, spaces):
        pl.semaphore_signal(barrier, inc=1, device_id={"space": mate(step)}, device_id_type=MESH)

    def greet(step, carry):
        pl.semaphore_signal(barrier, inc=1, device_id={"snap": peer(step)}, device_id_type=MESH)
        return carry

    lax.fori_loop(1, groups, greet, 0)

    stretch = 3 * rows_y * cells_x

    def widen(snap, carry):
        start = pl.multiple_of(snap * stretch, stretch)
        velf[pl.ds(start, stretch), :] = vel_ref[snap].reshape(stretch, cells_z).astype(F32)
        return carry

    load_velocity.wait()
    lax.fori_loop(0, here, widen, 0)

    def tile(comp, x):
        pieces = [
            velf[pl.ds((comp * rows_y + y) * cells_x + x, here, stride=stretch), :]
            for y in range(rows_y)
        ]
        return jnp.concatenate(pieces, axis=0).astype(BF16)

    def target(step):
        mine = me // half
        far = (1 - mine) * half + lax.rem(me + step, half)
        near = mine * half + lax.rem(me + step, half)
        return jnp.where(step < half, far, near)

    def regroup(to, u_to, vw_to):
        start = to * width_x
        for x in range(width_x):
            u_to[x] = tile(0, start + x)
        for comp in range(2):
            for x in range(width_x + 2):
                vw_to[comp, x] = tile(comp + 1, lax.rem(start + x + cells_x - 1, cells_x))

    pl.semaphore_wait(barrier, groups + spaces - 2)

    def lead_copy(step):
        return pltpu.make_async_remote_copy(
            lead.at[me], lead.at[me],
            sem_lead_s.at[step], sem_lead_r.at[me], device_id={"snap": peer(step)}, device_id_type=MESH,
        )

    def copies(step):
        to = target(step)
        return (
            pltpu.make_async_remote_copy(
                send_vw.at[step], recv_vw.at[me],
                sem_vw_s.at[step], sem_vw_r.at[me], device_id={"snap": to}, device_id_type=MESH,
            ),
            pltpu.make_async_remote_copy(
                send_u.at[step], recv_u.at[me],
                sem_u_s.at[step], sem_u_r.at[me], device_id={"snap": to}, device_id_type=MESH,
            ),
        )

    def arrivals(source):
        return (
            pltpu.make_async_remote_copy(
                recv_vw.at[source], recv_vw.at[source],
                sem_vw_s.at[0], sem_vw_r.at[source], device_id={"snap": source}, device_id_type=MESH,
            ),
            pltpu.make_async_remote_copy(
                recv_u.at[source], recv_u.at[source],
                sem_u_s.at[0], sem_u_r.at[source], device_id={"snap": source}, device_id_type=MESH,
            ),
            pltpu.make_async_remote_copy(
                lead.at[source], lead.at[source],
                sem_lead_s.at[0], sem_lead_r.at[source], device_id={"snap": source}, device_id_type=MESH,
            ),
        )

    def launch(step, carry):
        regroup(target(step), send_u.at[step], send_vw.at[step])
        for copy in copies(step):
            copy.start()
        return carry

    lax.fori_loop(0, half, launch, 0)
    lax.fori_loop(half + 1, groups, launch, 0)
    regroup(me, recv_u.at[me], recv_vw.at[me])

    lead_width = lead.shape[2]
    turn = rot_ref[me // 2].T
    pick = (order_ref[me // 2] - me % 2).astype(F32)
    pick = pick * pick
    turn_own = turn[:rank] * (1.0 - pick) + turn[rank:] * pick
    lead_own = exact(leaf_ref[0], turn_own)
    repeat = (iota((rank, lead_width), 1) % rank == iota((rank, lead_width), 0)).astype(F32)
    lead_wide = exact(lead_own, repeat)
    lead[me] = jnp.where(iota(lead_wide.shape, 1) // rank == me // 2, lead_wide, 0.0)

    def launch_lead(step, carry):
        lead_copy(step).start()
        return carry

    lax.fori_loop(1, groups, launch_lead, 0)

    def halo_copy(side, group):
        to = sp + 1 if side == 0 else sp - 1
        return pltpu.make_async_remote_copy(
            stage.at[side, group], halo.at[side, group],
            sem_halo_s.at[side, group], sem_halo_r.at[side, group],
            device_id={"space": to}, device_id_type=MESH,
        )

    def forward(group):
        for x in range(width_x):
            u_here = recv_u[group, x].astype(F32)
            w_here = recv_vw[group, 1, x + 1].astype(F32)
            stage[1, group, x] = jnp.concatenate([u_here[:here], w_here[:here]], axis=0).astype(BF16)
            stage[0, group, x] = jnp.concatenate([u_here[-here:], w_here[-here:]], axis=0).astype(BF16)

        @pl.when(sp < spaces - 1)
        def _():
            halo_copy(0, group).start()

        @pl.when(sp > 0)
        def _():
            halo_copy(1, group).start()

    @pl.when(sp == 0)
    def _():
        halo[0] = jnp.zeros(halo.shape[1:], BF16)

    @pl.when(sp == spaces - 1)
    def _():
        halo[1] = jnp.zeros(halo.shape[1:], BF16)

    for y in range(rows_y):
        for x in range(width_x):
            ids = block_ref[y, pl.ds(first_x + x, 1), :]
            for axis in range(3):
                value = jnp.zeros((1, cells_z), F32)
                for block in range(blocks):
                    value = jnp.where(ids == block, metric_ref[axis, block], value)
                spacing[axis, y, pl.ds(x, 1), :] = 0.5 * value

    plane = cells_x * cells_z
    rest = parts.shape[0] - 2 * total
    parts[pl.ds(2 * total, rest), :] = jnp.zeros((rest, parts.shape[1]), BF16)
    row = iota((rank, cells_z), 0)
    wanted = jnp.zeros((rank, cells_z), jnp.int32)
    for mode in range(rank):
        wanted = jnp.where(row == mode, cell_ref[mode], wanted)
    for comp in range(3):
        for y in range(rows_y):
            for x in range(width_x):
                base = ((comp * rows_y * spaces + sp * rows_y + y) * cells_x + first_x + x) * cells_z
                hit = jnp.where(wanted == base + iota((rank, cells_z), 1), 1.0, 0.0)
                column = ((comp * rows_y + y) * width_x + x) * cells_z
                parts[pl.ds(2 * total, rank), pl.ds(column, cells_z)] = hit.astype(BF16)

    depth = groups.bit_length() - 1
    turns = []
    for level in range(1, depth):
        nodes = groups >> level + 1
        stacked = []
        for k in range(nodes):
            node = groups - (groups >> level) + k
            plain = rot_ref[node].T
            swapped = jnp.concatenate([plain[rank:], plain[:rank]], axis=0)
            flag = order_ref[node].astype(F32)
            stacked.append(plain * (1.0 - flag) + swapped * flag)
        stacked = stacked[0] if nodes == 1 else jnp.concatenate(stacked, axis=0)
        if nodes > 1:
            shape = (rank, rank * nodes)
            copy_out = (iota(shape, 1) % rank == iota(shape, 0)).astype(F32)
            stacked = exact(stacked, copy_out)
            stacked = jnp.where(
                iota(stacked.shape, 0) // (2 * rank) == iota(stacked.shape, 1) // rank, stacked, 0.0
            )
        turns.append(stacked)

    def split_store(start, column, value):
        high, low = split(value)
        parts[pl.ds(start, 2 * here), pl.ds(column, cells_z)] = low
        parts[pl.ds(total + start, 2 * here), pl.ds(column, cells_z)] = high

    def wait_halo(group):
        @pl.when(sp > 0)
        def _():
            halo_copy(0, group).wait_recv()

        @pl.when(sp < spaces - 1)
        def _():
            halo_copy(1, group).wait_recv()

    def curl(pair):
        pair_groups = (2 * pair, 2 * pair + 1)
        start = pl.multiple_of(pair * 2 * here, 2 * here)
        for group in pair_groups:
            wait_halo(group)

        def load(ref, *index):
            both = [ref[(group, *index)].astype(F32) for group in pair_groups]
            return [
                jnp.concatenate([item[y * here:(y + 1) * here] for item in both], axis=0)
                for y in range(rows_y)
            ]

        def load_halo(side, x):
            both = [halo[side, group, x].astype(F32) for group in pair_groups]
            return [jnp.concatenate([item[c * here:(c + 1) * here] for item in both], axis=0) for c in range(2)]

        def along_z(field):
            return pltpu.roll(field, cells_z - 1, 1) - pltpu.roll(field, 1, 1)

        for x in range(width_x):
            u_at = load(recv_u, x)
            v_at = load(recv_vw, 0, x + 1)
            w_at = load(recv_vw, 1, x + 1)
            v_ends = load(recv_vw, 0, x), load(recv_vw, 0, x + 2)
            w_ends = load(recv_vw, 1, x), load(recv_vw, 1, x + 2)
            below = load_halo(0, x)
            above = load_halo(1, x)
            for y in range(rows_y):
                hx, hy, hz = (spacing[axis, y, pl.ds(x, 1), :] for axis in range(3))
                u_down = u_at[y - 1] if y > 0 else below[0]
                w_down = w_at[y - 1] if y > 0 else below[1]
                u_up = u_at[y + 1] if y < rows_y - 1 else above[0]
                w_up = w_at[y + 1] if y < rows_y - 1 else above[1]
                omega = (
                    hy * (w_up - w_down) - hz * along_z(v_at[y]),
                    hz * along_z(u_at[y]) - hx * (w_ends[1][y] - w_ends[0][y]),
                    hx * (v_ends[1][y] - v_ends[0][y]) - hy * (u_up - u_down),
                )
                for comp in range(3):
                    split_store(start, ((comp * rows_y + y) * width_x + x) * cells_z, omega[comp])

    def nth_pair(step):
        quarter = max(half // 2, 1)
        own = me // 2
        side = own // quarter
        near = side * quarter + lax.rem(own + step, quarter)
        far = (1 - side) * quarter + lax.rem(own + step, quarter)
        return jnp.where(step < quarter, near, far) if half > 1 else own

    def pipeline(step, carry):
        @pl.when(step < half)
        def _():
            for place in range(2):
                source = 2 * nth_pair(step) + place

                @pl.when(source != me)
                def _():
                    for copy in arrivals(source):
                        copy.wait_recv()

                forward(source)

        @pl.when(step > 0)
        def _():
            curl(nth_pair(step - 1))

        return carry

    lax.fori_loop(0, half + 1, pipeline, 0)

    both = product(parts[:2 * total], parts[total:], ((1,), (1,)))
    crossed = both[:total, :total].T
    gap = jnp.zeros((total, both.shape[1] - total), F32)
    gram_own[...] = (both[:total] + both[total:] + jnp.concatenate([crossed, gap], axis=1)).reshape(gram_own.shape)

    def copy_a(step):
        to = mate(step)
        return pltpu.make_async_remote_copy(
            gram_own.at[to], gram_space.at[step], sem_a_s.at[step], sem_a_r.at[step],
            device_id={"space": to}, device_id_type=MESH,
        )

    for step in range(1, spaces):
        copy_a(step).start()
    lead_all = lead[...].reshape(total, lead_width)[:, :rank * groups // 2]
    part = gram_own[sp]
    for step in range(1, spaces):
        copy_a(step).wait_recv()
        part = part + gram_space[step]
    gram_snap[0] = part

    def copy_b(step):
        return pltpu.make_async_remote_copy(
            gram_snap.at[0], gram_snap.at[step], sem_b_s.at[step], sem_b_r.at[step],
            device_id={"snap": peer(step)}, device_id_type=MESH,
        )

    def start_b(step, carry):
        copy_b(step).start()
        return carry

    def finish_b(step, carry):
        copy_b(step).wait_recv()
        return carry + gram_snap[step]

    lax.fori_loop(1, groups, start_b, 0)
    gram_all[sp] = lax.fori_loop(1, groups, finish_b, part)

    def copy_c(step, owner):
        return pltpu.make_async_remote_copy(
            gram_all.at[owner], gram_all.at[owner], sem_c_s.at[step], sem_c_r.at[step],
            device_id={"space": mate(step)}, device_id_type=MESH,
        )

    for step in range(1, spaces):
        copy_c(step, sp).start()
    for step in range(1, spaces):
        copy_c(step, lax.rem(sp - step + spaces, spaces)).wait_recv()
    summed = gram_all[...].reshape(total, gram_all.shape[2])

    entries = summed[:, total:total + rank]
    maps = lead_all
    gram = close(maps.T, close(summed[:, :total], maps))
    for turn in turns:
        step_map = close(ortho_factor(gram, rank), turn)
        gram = close(step_map.T, close(gram, step_map))
        maps = close(maps, step_map)
    factor = ortho_factor(gram, rank)
    value = jnp.sum(factor * close(maps.T, entries), axis=0, keepdims=True)
    norm_sq = jnp.sum(factor * close(gram, factor), axis=0, keepdims=True)
    cells_all = 3 * rows_y * spaces * plane
    floor = 0.5 * jnp.sqrt(norm_sq / cells_all + 1e-06)
    sign = value / jnp.maximum(jnp.abs(value), floor)
    mix = close((factor * sign).T, maps, ((1,), (1,)))
    mix_high, mix_low = split(mix)
    high = parts[total:2 * total]
    both = product(jnp.concatenate([mix_high, mix_low], axis=0), high)
    out_ref[...] = both[:rank] + both[rank:] + product(mix_high, parts[:total])

    def finish(step, carry):
        for copy in copies(step):
            copy.wait_send()
        return carry

    lax.fori_loop(0, half, finish, 0)
    lax.fori_loop(half + 1, groups, finish, 0)

    def finish_small(step, carry):
        lead_copy(step).wait_send()
        copy_b(step).wait_send()
        return carry

    lax.fori_loop(1, groups, finish_small, 0)
    for step in range(1, spaces):
        copy_a(step).wait_send()
        copy_c(step, sp).wait_send()

    def finish_halo(group, carry):
        @pl.when(sp < spaces - 1)
        def _():
            halo_copy(0, group).wait_send()

        @pl.when(sp > 0)
        def _():
            halo_copy(1, group).wait_send()

        return carry

    lax.fori_loop(0, groups, finish_halo, 0)


def padded(size, unit):
    return -(-size // unit) * unit


def local(velocity, block_id, metric, leaf_rot, merge_rot, merge_order, ref_cell):
    here, _, rows_y, cells_x, cells_z = velocity.shape
    rank = leaf_rot.shape[2]
    groups = lax.axis_size("snap")
    spaces = lax.axis_size("space")
    total = groups * here
    width_x = cells_x // groups
    tile_rows = rows_y * here
    cells = 3 * rows_y * width_x * cells_z
    gram_width = padded(total + rank, 128)
    share = total // spaces
    lead_width = padded(rank * groups // 2, 128)
    vmem = pl.BlockSpec(memory_space=pltpu.VMEM)
    smem = pl.BlockSpec(memory_space=pltpu.SMEM)
    dma = pltpu.SemaphoreType.DMA
    modes = pl.pallas_call(
        functools.partial(kernel, (groups, spaces)),
        out_shape=jax.ShapeDtypeStruct((rank, cells), F32),
        in_specs=[pl.BlockSpec(memory_space=pltpu.HBM), vmem, smem, vmem, vmem, smem, smem],
        out_specs=vmem,
        scratch_shapes=[
            pltpu.VMEM(velocity.shape, BF16),
            pltpu.VMEM((here * 3 * rows_y * cells_x, cells_z), F32),
            pltpu.VMEM((groups, width_x, tile_rows, cells_z), BF16),
            pltpu.VMEM((groups, 2, width_x + 2, tile_rows, cells_z), BF16),
            pltpu.VMEM((groups, width_x, tile_rows, cells_z), BF16),
            pltpu.VMEM((groups, 2, width_x + 2, tile_rows, cells_z), BF16),
            pltpu.VMEM((2, groups, width_x, 2 * here, cells_z), BF16),
            pltpu.VMEM((2, groups, width_x, 2 * here, cells_z), BF16),
            pltpu.VMEM((groups, here, lead_width), F32),
            pltpu.VMEM((3, rows_y, width_x, cells_z), F32),
            pltpu.VMEM((total + gram_width, cells), BF16),
            pltpu.VMEM((spaces, share, gram_width), F32),
            pltpu.VMEM((spaces, share, gram_width), F32),
            pltpu.VMEM((groups, share, gram_width), F32),
            pltpu.VMEM((spaces, share, gram_width), F32),
        ]
        + [dma]
        + [dma((groups,))] * 6
        + [dma((2, groups))] * 2
        + [dma((spaces,))] * 2
        + [dma((groups,))] * 2
        + [dma((spaces,))] * 2,
        compiler_params=pltpu.CompilerParams(
            collective_id=0, has_side_effects=True, vmem_limit_bytes=32 * 1024 * 1024
        ),
    )(velocity, block_id, metric.T, leaf_rot, jnp.swapaxes(merge_rot, 1, 2), merge_order, ref_cell)
    return modes.reshape(rank, 3, rows_y, width_x * cells_z)


def solution(mesh):
    placed = (
        P("snap", None, "space", None, None),
        P("space", None, None),
        P(),
        P("snap", None, None),
        P(),
        P(),
        P(),
    )
    return jax.shard_map(
        local, mesh=mesh, in_specs=placed, out_specs=P(None, None, "space", "snap"), check_vma=False
    )
```

```python
import functools

import jax
import jax.numpy as jnp
from jax import lax
from jax.experimental import pallas as pl
from jax.experimental.pallas import tpu as pltpu
from jax.sharding import PartitionSpec as P

HIGHEST = lax.Precision.HIGHEST
MESH = pl.DeviceIdType.MESH
F32 = jnp.float32
BF16 = jnp.bfloat16


def exact(left, right, dims=((1,), (0,))):
    return lax.dot_general(left, right, (dims, ((), ())), precision=HIGHEST, preferred_element_type=F32)


def product(left, right, dims=((1,), (0,))):
    return lax.dot_general(left, right, (dims, ((), ())), preferred_element_type=F32)


def split(value):
    high = value.astype(BF16)
    return high, (value - high.astype(F32)).astype(BF16)


def iota(shape, dim):
    return lax.broadcasted_iota(jnp.int32, shape, dim)


def ortho_factor(gram, rank):
    size = gram.shape[0]
    eye = iota(gram.shape, 0) == iota(gram.shape, 1)
    same = iota(gram.shape, 0) // rank == iota(gram.shape, 1) // rank
    diagonal = jnp.sum(jnp.where(eye, gram, 0.0), axis=0, keepdims=True)
    node_of = iota((1, size), 1) // rank
    trace = jnp.zeros((1, size), F32)
    for node in range(size // rank):
        own = jnp.where(node_of == node, diagonal, 0.0)
        trace = jnp.where(node_of == node, jnp.sum(own, axis=1, keepdims=True), trace)
    scale = (trace + 1e-06) / rank
    return 1.5 * eye.astype(F32) - jnp.where(same, 0.5 * gram / scale, 0.0)


def kernel(
    dims,
    vel_hbm, block_hbm, metric_hbm, leaf_hbm, rot_hbm, order_hbm, cell_hbm, out_ref,
    vel_ref, block_ref, metric_ref, leaf_ref, rot_ref, order_ref, cell_ref,
    velf, send, recv, stage, halo, lead, spacing, parts,
    gram_own, gram_space, gram_snap, gram_all,
    sem_in, sem_main_s, sem_main_r, sem_x_s, sem_x_r, sem_lead_s, sem_lead_r, sem_halo_s, sem_halo_r,
    sem_a_s, sem_a_r, sem_b_s, sem_b_r, sem_c_s, sem_c_r,
):
    groups, spaces = dims
    here, _, rows_y, cells_x, cells_z = vel_ref.shape
    rank = leaf_ref.shape[2]
    blocks = metric_ref.shape[1]
    total = groups * here
    width_x = cells_x // groups
    me = lax.axis_index("snap")
    sp = lax.axis_index("space")
    first_x = me * width_x

    half = groups // 2
    loads = [
        pltpu.make_async_copy(source, place, sem_in.at[index])
        for index, (source, place) in enumerate((
            (vel_hbm, vel_ref), (block_hbm, block_ref), (metric_hbm, metric_ref), (leaf_hbm, leaf_ref),
            (rot_hbm, rot_ref), (order_hbm, order_ref), (cell_hbm, cell_ref),
        ))
    ]
    for load in loads:
        load.start()

    def peer(step):
        return lax.rem(me + step, groups)

    def mate(step):
        return lax.rem(sp + step, spaces)

    barrier = pltpu.get_barrier_semaphore()
    for step in range(1, spaces):
        pl.semaphore_signal(barrier, inc=1, device_id={"space": mate(step)}, device_id_type=MESH)

    def greet(step, carry):
        pl.semaphore_signal(barrier, inc=1, device_id={"snap": peer(step)}, device_id_type=MESH)
        return carry

    lax.fori_loop(1, groups, greet, 0)

    stretch = 3 * rows_y * cells_x

    def widen(snap, carry):
        start = pl.multiple_of(snap * stretch, stretch)
        velf[pl.ds(start, stretch), :] = vel_ref[snap].reshape(stretch, cells_z).astype(F32)
        return carry

    loads[0].wait()
    lax.fori_loop(0, here, widen, 0)

    def tile(comp, x):
        pieces = [
            velf[pl.ds((comp * rows_y + y) * cells_x + x, here, stride=stretch), :]
            for y in range(rows_y)
        ]
        return jnp.concatenate(pieces, axis=0).astype(BF16)

    def target(step):
        mine = me // half
        far = (1 - mine) * half + lax.rem(me + step, half)
        near = mine * half + lax.rem(me + step, half)
        return jnp.where(step < half, far, near)

    def regroup(to, place):
        start = to * width_x
        for comp in range(3):
            for x in range(width_x):
                place[comp, x] = tile(comp, start + x)

    pl.semaphore_wait(barrier, groups + spaces - 2)

    def lead_copy(step):
        return pltpu.make_async_remote_copy(
            lead.at[me], lead.at[me],
            sem_lead_s.at[step], sem_lead_r.at[me], device_id={"snap": peer(step)}, device_id_type=MESH,
        )

    def main_copy(step):
        return pltpu.make_async_remote_copy(
            send.at[step], recv.at[me, :, pl.ds(1, width_x)],
            sem_main_s.at[step], sem_main_r.at[me], device_id={"snap": target(step)}, device_id_type=MESH,
        )

    def x_copy(side, group):
        from_row, to_row = (width_x, 0) if side == 0 else (1, width_x + 1)
        to = peer(1) if side == 0 else peer(groups - 1)
        return pltpu.make_async_remote_copy(
            recv.at[group, pl.ds(1, 2), from_row], recv.at[group, pl.ds(1, 2), to_row],
            sem_x_s.at[side, group], sem_x_r.at[side, group], device_id={"snap": to}, device_id_type=MESH,
        )

    def arrivals(source):
        return (
            pltpu.make_async_remote_copy(
                recv.at[source, :, pl.ds(1, width_x)], recv.at[source, :, pl.ds(1, width_x)],
                sem_main_s.at[0], sem_main_r.at[source], device_id={"snap": source}, device_id_type=MESH,
            ),
            pltpu.make_async_remote_copy(
                lead.at[source], lead.at[source],
                sem_lead_s.at[0], sem_lead_r.at[source], device_id={"snap": source}, device_id_type=MESH,
            ),
        )

    def launch(step, carry):
        regroup(target(step), send.at[step])
        main_copy(step).start()
        return carry

    lax.fori_loop(0, half, launch, 0)
    lax.fori_loop(half + 1, groups, launch, 0)
    regroup(me, recv.at[me, :, pl.ds(1, width_x)])
    for load in loads[1:]:
        load.wait()

    lead_width = lead.shape[2]
    turn = rot_ref[me // 2].T
    pick = (order_ref[me // 2] - me % 2).astype(F32)
    pick = pick * pick
    turn_own = turn[:rank] * (1.0 - pick) + turn[rank:] * pick
    lead_own = exact(leaf_ref[0], turn_own)
    repeat = (iota((rank, lead_width), 1) % rank == iota((rank, lead_width), 0)).astype(F32)
    lead_wide = exact(lead_own, repeat)
    lead[me] = jnp.where(iota(lead_wide.shape, 1) // rank == me // 2, lead_wide, 0.0)

    def launch_lead(step, carry):
        lead_copy(step).start()
        return carry

    lax.fori_loop(1, groups, launch_lead, 0)

    def halo_copy(side, group):
        to = sp + 1 if side == 0 else sp - 1
        return pltpu.make_async_remote_copy(
            stage.at[side, group], halo.at[side, group],
            sem_halo_s.at[side, group], sem_halo_r.at[side, group],
            device_id={"space": to}, device_id_type=MESH,
        )

    def forward(group):
        for side in range(2):
            x_copy(side, group).start()
        for x in range(width_x):
            u_here = recv[group, 0, x + 1].astype(F32)
            w_here = recv[group, 2, x + 1].astype(F32)
            stage[1, group, x] = jnp.concatenate([u_here[:here], w_here[:here]], axis=0).astype(BF16)
            stage[0, group, x] = jnp.concatenate([u_here[-here:], w_here[-here:]], axis=0).astype(BF16)

        @pl.when(sp < spaces - 1)
        def _():
            halo_copy(0, group).start()

        @pl.when(sp > 0)
        def _():
            halo_copy(1, group).start()

    @pl.when(sp == 0)
    def _():
        halo[0] = jnp.zeros(halo.shape[1:], BF16)

    @pl.when(sp == spaces - 1)
    def _():
        halo[1] = jnp.zeros(halo.shape[1:], BF16)

    for y in range(rows_y):
        for x in range(width_x):
            ids = block_ref[y, pl.ds(first_x + x, 1), :]
            for axis in range(3):
                value = jnp.zeros((1, cells_z), F32)
                for block in range(blocks):
                    value = jnp.where(ids == block, metric_ref[axis, block], value)
                spacing[axis, y, pl.ds(x, 1), :] = 0.5 * value

    plane = cells_x * cells_z
    rest = parts.shape[0] - 2 * total
    parts[pl.ds(2 * total, rest), :] = jnp.zeros((rest, parts.shape[1]), BF16)
    row = iota((rank, cells_z), 0)
    wanted = jnp.zeros((rank, cells_z), jnp.int32)
    for mode in range(rank):
        wanted = jnp.where(row == mode, cell_ref[mode], wanted)
    for comp in range(3):
        for y in range(rows_y):
            for x in range(width_x):
                base = ((comp * rows_y * spaces + sp * rows_y + y) * cells_x + first_x + x) * cells_z
                hit = jnp.where(wanted == base + iota((rank, cells_z), 1), 1.0, 0.0)
                column = ((comp * rows_y + y) * width_x + x) * cells_z
                parts[pl.ds(2 * total, rank), pl.ds(column, cells_z)] = hit.astype(BF16)

    depth = groups.bit_length() - 1
    turns = []
    for level in range(1, depth):
        nodes = groups >> level + 1
        stacked = []
        for k in range(nodes):
            node = groups - (groups >> level) + k
            plain = rot_ref[node].T
            swapped = jnp.concatenate([plain[rank:], plain[:rank]], axis=0)
            flag = order_ref[node].astype(F32)
            stacked.append(plain * (1.0 - flag) + swapped * flag)
        stacked = stacked[0] if nodes == 1 else jnp.concatenate(stacked, axis=0)
        if nodes > 1:
            shape = (rank, rank * nodes)
            copy_out = (iota(shape, 1) % rank == iota(shape, 0)).astype(F32)
            stacked = exact(stacked, copy_out)
            stacked = jnp.where(
                iota(stacked.shape, 0) // (2 * rank) == iota(stacked.shape, 1) // rank, stacked, 0.0
            )
        turns.append(stacked)

    def split_store(start, column, value):
        high, low = split(value)
        parts[pl.ds(start, 2 * here), pl.ds(column, cells_z)] = low
        parts[pl.ds(total + start, 2 * here), pl.ds(column, cells_z)] = high

    def wait_halo(group):
        for side in range(2):
            x_copy(side, group).wait_recv()

        @pl.when(sp > 0)
        def _():
            halo_copy(0, group).wait_recv()

        @pl.when(sp < spaces - 1)
        def _():
            halo_copy(1, group).wait_recv()

    def curl(pair):
        pair_groups = (2 * pair, 2 * pair + 1)
        start = pl.multiple_of(pair * 2 * here, 2 * here)
        for group in pair_groups:
            wait_halo(group)

        def load(ref, *index):
            both = [ref[(group, *index)].astype(F32) for group in pair_groups]
            return [
                jnp.concatenate([item[y * here:(y + 1) * here] for item in both], axis=0)
                for y in range(rows_y)
            ]

        def load_halo(side, x):
            both = [halo[side, group, x].astype(F32) for group in pair_groups]
            return [jnp.concatenate([item[c * here:(c + 1) * here] for item in both], axis=0) for c in range(2)]

        def along_z(field):
            return pltpu.roll(field, cells_z - 1, 1) - pltpu.roll(field, 1, 1)

        for x in range(width_x):
            u_at = load(recv, 0, x + 1)
            v_at = load(recv, 1, x + 1)
            w_at = load(recv, 2, x + 1)
            v_ends = load(recv, 1, x), load(recv, 1, x + 2)
            w_ends = load(recv, 2, x), load(recv, 2, x + 2)
            below = load_halo(0, x)
            above = load_halo(1, x)
            for y in range(rows_y):
                hx, hy, hz = (spacing[axis, y, pl.ds(x, 1), :] for axis in range(3))
                u_down = u_at[y - 1] if y > 0 else below[0]
                w_down = w_at[y - 1] if y > 0 else below[1]
                u_up = u_at[y + 1] if y < rows_y - 1 else above[0]
                w_up = w_at[y + 1] if y < rows_y - 1 else above[1]
                omega = (
                    hy * (w_up - w_down) - hz * along_z(v_at[y]),
                    hz * along_z(u_at[y]) - hx * (w_ends[1][y] - w_ends[0][y]),
                    hx * (v_ends[1][y] - v_ends[0][y]) - hy * (u_up - u_down),
                )
                for comp in range(3):
                    split_store(start, ((comp * rows_y + y) * width_x + x) * cells_z, omega[comp])

    quarter = half // 2
    near = me // half * quarter
    far = quarter - near

    def take(pair):
        for place in range(2):
            source = 2 * pair + place

            @pl.when(source != me)
            def _():
                for copy in arrivals(source):
                    copy.wait_recv()

            forward(source)

    def take_near(step, carry):
        take(near + step)
        return carry

    def take_far(step, carry):
        take(far + step)
        curl(near + step)
        return carry

    def curl_far(step, carry):
        curl(far + step)
        return carry

    lax.fori_loop(0, quarter, take_near, 0)
    lax.fori_loop(0, quarter, take_far, 0)
    lax.fori_loop(0, quarter, curl_far, 0)

    both = product(parts[:2 * total], parts[total:], ((1,), (1,)))
    crossed = both[:total, :total].T
    gap = jnp.zeros((total, both.shape[1] - total), F32)
    gram_own[...] = (both[:total] + both[total:] + jnp.concatenate([crossed, gap], axis=1)).reshape(gram_own.shape)

    def copy_a(step):
        to = mate(step)
        return pltpu.make_async_remote_copy(
            gram_own.at[to], gram_space.at[step], sem_a_s.at[step], sem_a_r.at[step],
            device_id={"space": to}, device_id_type=MESH,
        )

    for step in range(1, spaces):
        copy_a(step).start()
    lead_all = lead[...].reshape(total, lead_width)[:, :rank * groups // 2]
    part = gram_own[sp]
    for step in range(1, spaces):
        copy_a(step).wait_recv()
        part = part + gram_space[step]
    gram_snap[0] = part

    def copy_b(step):
        return pltpu.make_async_remote_copy(
            gram_snap.at[0], gram_snap.at[step], sem_b_s.at[step], sem_b_r.at[step],
            device_id={"snap": peer(step)}, device_id_type=MESH,
        )

    def start_b(step, carry):
        copy_b(step).start()
        return carry

    def finish_b(step, carry):
        copy_b(step).wait_recv()
        return carry + gram_snap[step]

    lax.fori_loop(1, groups, start_b, 0)
    gram_all[sp] = lax.fori_loop(1, groups, finish_b, part)

    def copy_c(step, owner):
        return pltpu.make_async_remote_copy(
            gram_all.at[owner], gram_all.at[owner], sem_c_s.at[step], sem_c_r.at[step],
            device_id={"space": mate(step)}, device_id_type=MESH,
        )

    for step in range(1, spaces):
        copy_c(step, sp).start()
    for step in range(1, spaces):
        copy_c(step, lax.rem(sp - step + spaces, spaces)).wait_recv()
    summed = gram_all[...].reshape(total, gram_all.shape[2])

    entries = summed[:, total:total + rank]
    maps = lead_all
    gram = exact(maps.T, exact(summed[:, :total], maps))
    for turn in turns:
        step_map = exact(ortho_factor(gram, rank), turn)
        gram = exact(step_map.T, exact(gram, step_map))
        maps = exact(maps, step_map)
    factor = ortho_factor(gram, rank)
    value = jnp.sum(factor * exact(entries.T, maps), axis=1, keepdims=True)
    norm_sq = jnp.sum(factor * exact(factor, gram), axis=1, keepdims=True)
    cells_all = 3 * rows_y * spaces * plane
    floor = 0.5 * jnp.sqrt(norm_sq / cells_all + 1e-06)
    sign = value / jnp.maximum(jnp.abs(value), floor)
    mix = exact(factor, maps.T)
    mix_high, mix_low = split(mix)
    high = parts[total:2 * total]
    both = product(jnp.concatenate([mix_high, mix_low], axis=0), high)
    out_ref[...] = (both[:rank] + both[rank:] + product(mix_high, parts[:total])) * sign

    def finish(step, carry):
        main_copy(step).wait_send()
        return carry

    lax.fori_loop(0, half, finish, 0)
    lax.fori_loop(half + 1, groups, finish, 0)

    def finish_small(step, carry):
        lead_copy(step).wait_send()
        copy_b(step).wait_send()
        return carry

    lax.fori_loop(1, groups, finish_small, 0)
    for step in range(1, spaces):
        copy_a(step).wait_send()
        copy_c(step, sp).wait_send()

    def finish_halo(group, carry):
        for side in range(2):
            x_copy(side, group).wait_send()

        @pl.when(sp < spaces - 1)
        def _():
            halo_copy(0, group).wait_send()

        @pl.when(sp > 0)
        def _():
            halo_copy(1, group).wait_send()

        return carry

    lax.fori_loop(0, groups, finish_halo, 0)


def padded(size, unit):
    return -(-size // unit) * unit


def local(velocity, block_id, metric, leaf_rot, merge_rot, merge_order, ref_cell):
    here, _, rows_y, cells_x, cells_z = velocity.shape
    rank = leaf_rot.shape[2]
    groups = lax.axis_size("snap")
    spaces = lax.axis_size("space")
    total = groups * here
    width_x = cells_x // groups
    tile_rows = rows_y * here
    cells = 3 * rows_y * width_x * cells_z
    gram_width = padded(total + rank, 128)
    share = total // spaces
    lead_width = padded(rank * groups // 2, 128)
    vmem = pl.BlockSpec(memory_space=pltpu.VMEM)
    dma = pltpu.SemaphoreType.DMA
    modes = pl.pallas_call(
        functools.partial(kernel, (groups, spaces)),
        out_shape=jax.ShapeDtypeStruct((rank, cells), F32),
        in_specs=[pl.BlockSpec(memory_space=pltpu.HBM)] * 7,
        out_specs=vmem,
        scratch_shapes=[
            pltpu.VMEM(velocity.shape, BF16),
            pltpu.VMEM(block_id.shape, jnp.int32),
            pltpu.SMEM(metric.shape[::-1], F32),
            pltpu.VMEM(leaf_rot.shape, F32),
            pltpu.VMEM((merge_rot.shape[0], rank, 2 * rank), F32),
            pltpu.SMEM(merge_order.shape, jnp.int32),
            pltpu.SMEM(ref_cell.shape, jnp.int32),
            pltpu.VMEM((here * 3 * rows_y * cells_x, cells_z), F32),
            pltpu.VMEM((groups, 3, width_x, tile_rows, cells_z), BF16),
            pltpu.VMEM((groups, 3, width_x + 2, tile_rows, cells_z), BF16),
            pltpu.VMEM((2, groups, width_x, 2 * here, cells_z), BF16),
            pltpu.VMEM((2, groups, width_x, 2 * here, cells_z), BF16),
            pltpu.VMEM((groups, here, lead_width), F32),
            pltpu.VMEM((3, rows_y, width_x, cells_z), F32),
            pltpu.VMEM((total + gram_width, cells), BF16),
            pltpu.VMEM((spaces, share, gram_width), F32),
            pltpu.VMEM((spaces, share, gram_width), F32),
            pltpu.VMEM((groups, share, gram_width), F32),
            pltpu.VMEM((spaces, share, gram_width), F32),
        ]
        + [dma((7,))]
        + [dma((groups,))] * 2
        + [dma((2, groups))] * 2
        + [dma((groups,))] * 2
        + [dma((2, groups))] * 2
        + [dma((spaces,))] * 2
        + [dma((groups,))] * 2
        + [dma((spaces,))] * 2,
        compiler_params=pltpu.CompilerParams(
            collective_id=0, has_side_effects=True, vmem_limit_bytes=56 * 1024 * 1024
        ),
    )(velocity, block_id, metric.T, leaf_rot, jnp.swapaxes(merge_rot, 1, 2), merge_order, ref_cell)
    return modes.reshape(rank, 3, rows_y, width_x * cells_z)


def solution(mesh):
    placed = (
        P("snap", None, "space", None, None),
        P("space", None, None),
        P(),
        P("snap", None, None),
        P(),
        P(),
        P(),
    )
    return jax.shard_map(
        local, mesh=mesh, in_specs=placed, out_specs=P(None, None, "space", "snap"), check_vma=False
    )
```

```python
import functools

import jax
import jax.numpy as jnp
from jax import lax
from jax.experimental import pallas as pl
from jax.experimental.pallas import tpu as pltpu
from jax.sharding import PartitionSpec as P

HIGHEST = lax.Precision.HIGHEST
MESH = pl.DeviceIdType.MESH
F32 = jnp.float32
BF16 = jnp.bfloat16


def exact(left, right, dims=((1,), (0,))):
    return lax.dot_general(left, right, (dims, ((), ())), precision=HIGHEST, preferred_element_type=F32)


def product(left, right, dims=((1,), (0,))):
    return lax.dot_general(left, right, (dims, ((), ())), preferred_element_type=F32)


def split(value):
    high = value.astype(BF16)
    return high, (value - high.astype(F32)).astype(BF16)


def iota(shape, dim):
    return lax.broadcasted_iota(jnp.int32, shape, dim)


def ortho_factor(gram, rank):
    size = gram.shape[0]
    eye = iota(gram.shape, 0) == iota(gram.shape, 1)
    same = iota(gram.shape, 0) // rank == iota(gram.shape, 1) // rank
    diagonal = jnp.sum(jnp.where(eye, gram, 0.0), axis=0, keepdims=True)
    node_of = iota((1, size), 1) // rank
    trace = jnp.zeros((1, size), F32)
    for node in range(size // rank):
        own = jnp.where(node_of == node, diagonal, 0.0)
        trace = jnp.where(node_of == node, jnp.sum(own, axis=1, keepdims=True), trace)
    scale = (trace + 1e-06) / rank
    return 1.5 * eye.astype(F32) - jnp.where(same, 0.5 * gram / scale, 0.0)


def kernel(
    dims,
    vel_hbm, block_hbm, metric_hbm, leaf_hbm, rot_hbm, order_hbm, cell_hbm, out_ref,
    vel_ref, block_ref, metric_ref, leaf_ref, rot_ref, order_ref, cell_ref,
    velf, send, recv, stage, halo, lead, spacing, parts,
    gram_own, gram_space, gram_snap, gram_all,
    sem_in, sem_main_s, sem_main_r, sem_x_s, sem_x_r, sem_lead_s, sem_lead_r, sem_halo_s, sem_halo_r,
    sem_a_s, sem_a_r, sem_b_s, sem_b_r, sem_c_s, sem_c_r,
):
    groups, spaces = dims
    here, _, rows_y, cells_x, cells_z = vel_ref.shape
    rank = leaf_ref.shape[2]
    blocks = metric_ref.shape[1]
    total = groups * here
    width_x = cells_x // groups
    me = lax.axis_index("snap")
    sp = lax.axis_index("space")
    first_x = me * width_x

    half = groups // 2
    loads = [
        pltpu.make_async_copy(source, place, sem_in.at[index])
        for index, (source, place) in enumerate((
            (vel_hbm, vel_ref), (block_hbm, block_ref), (metric_hbm, metric_ref), (leaf_hbm, leaf_ref),
            (rot_hbm, rot_ref), (order_hbm, order_ref), (cell_hbm, cell_ref),
        ))
    ]
    for load in loads:
        load.start()

    def peer(step):
        return lax.rem(me + step, groups)

    def mate(step):
        return lax.rem(sp + step, spaces)

    barrier = pltpu.get_barrier_semaphore()
    for step in range(1, spaces):
        pl.semaphore_signal(barrier, inc=1, device_id={"space": mate(step)}, device_id_type=MESH)

    def greet(step, carry):
        pl.semaphore_signal(barrier, inc=1, device_id={"snap": peer(step)}, device_id_type=MESH)
        return carry

    lax.fori_loop(1, groups, greet, 0)

    stretch = 3 * rows_y * cells_x

    def widen(snap, carry):
        start = pl.multiple_of(snap * stretch, stretch)
        velf[pl.ds(start, stretch), :] = vel_ref[snap].reshape(stretch, cells_z).astype(F32)
        return carry

    loads[0].wait()
    lax.fori_loop(0, here, widen, 0)

    def tile(comp, x):
        pieces = [
            velf[pl.ds((comp * rows_y + y) * cells_x + x, here, stride=stretch), :]
            for y in range(rows_y)
        ]
        return jnp.concatenate(pieces, axis=0).astype(BF16)

    def target(step):
        mine = me // half
        near = mine * half + lax.rem(me + step // 2, half)
        far = (1 - mine) * half + lax.rem(me + step // 2, half)
        return jnp.where(lax.rem(step, 2) == 0, near, far)

    def regroup(to, place):
        start = to * width_x
        for comp in range(3):
            for x in range(width_x):
                place[comp, x] = tile(comp, start + x)

    pl.semaphore_wait(barrier, groups + spaces - 2)

    def lead_copy(step):
        return pltpu.make_async_remote_copy(
            lead.at[me], lead.at[me],
            sem_lead_s.at[step], sem_lead_r.at[me], device_id={"snap": peer(step)}, device_id_type=MESH,
        )

    def main_copy(step):
        return pltpu.make_async_remote_copy(
            send.at[step], recv.at[me, :, pl.ds(1, width_x)],
            sem_main_s.at[step], sem_main_r.at[me], device_id={"snap": target(step)}, device_id_type=MESH,
        )

    def x_copy(side, pair):
        from_row, to_row = (width_x, 0) if side == 0 else (1, width_x + 1)
        to = peer(1) if side == 0 else peer(groups - 1)
        return pltpu.make_async_remote_copy(
            recv.at[pl.ds(2 * pair, 2), pl.ds(1, 2), from_row], recv.at[pl.ds(2 * pair, 2), pl.ds(1, 2), to_row],
            sem_x_s.at[side, pair], sem_x_r.at[side, pair], device_id={"snap": to}, device_id_type=MESH,
        )

    def arrivals(source):
        return (
            pltpu.make_async_remote_copy(
                recv.at[source, :, pl.ds(1, width_x)], recv.at[source, :, pl.ds(1, width_x)],
                sem_main_s.at[0], sem_main_r.at[source], device_id={"snap": source}, device_id_type=MESH,
            ),
            pltpu.make_async_remote_copy(
                lead.at[source], lead.at[source],
                sem_lead_s.at[0], sem_lead_r.at[source], device_id={"snap": source}, device_id_type=MESH,
            ),
        )

    def launch(step, carry):
        regroup(target(step), send.at[step])
        main_copy(step).start()
        return carry

    lax.fori_loop(1, groups, launch, 0)
    regroup(me, recv.at[me, :, pl.ds(1, width_x)])
    for load in loads[1:]:
        load.wait()

    lead_width = lead.shape[2]
    turn = rot_ref[me // 2].T
    pick = (order_ref[me // 2] - me % 2).astype(F32)
    pick = pick * pick
    turn_own = turn[:rank] * (1.0 - pick) + turn[rank:] * pick
    lead_own = exact(leaf_ref[0], turn_own)
    repeat = (iota((rank, lead_width), 1) % rank == iota((rank, lead_width), 0)).astype(F32)
    lead_wide = exact(lead_own, repeat)
    lead[me] = jnp.where(iota(lead_wide.shape, 1) // rank == me // 2, lead_wide, 0.0)

    def launch_lead(step, carry):
        lead_copy(step).start()
        return carry

    lax.fori_loop(1, groups, launch_lead, 0)

    def halo_copy(side, pair):
        to = sp + 1 if side == 0 else sp - 1
        return pltpu.make_async_remote_copy(
            stage.at[side, pl.ds(2 * pair, 2)], halo.at[side, pl.ds(2 * pair, 2)],
            sem_halo_s.at[side, pair], sem_halo_r.at[side, pair],
            device_id={"space": to}, device_id_type=MESH,
        )

    def forward(pair):
        for side in range(2):
            x_copy(side, pair).start()
        for place in range(2):
            group = 2 * pair + place
            for x in range(width_x):
                u_here = recv[group, 0, x + 1].astype(F32)
                w_here = recv[group, 2, x + 1].astype(F32)
                stage[1, group, x] = jnp.concatenate([u_here[:here], w_here[:here]], axis=0).astype(BF16)
                stage[0, group, x] = jnp.concatenate([u_here[-here:], w_here[-here:]], axis=0).astype(BF16)

        @pl.when(sp < spaces - 1)
        def _():
            halo_copy(0, pair).start()

        @pl.when(sp > 0)
        def _():
            halo_copy(1, pair).start()

    @pl.when(sp == 0)
    def _():
        halo[0] = jnp.zeros(halo.shape[1:], BF16)

    @pl.when(sp == spaces - 1)
    def _():
        halo[1] = jnp.zeros(halo.shape[1:], BF16)

    for y in range(rows_y):
        for x in range(width_x):
            ids = block_ref[y, pl.ds(first_x + x, 1), :]
            for axis in range(3):
                value = jnp.zeros((1, cells_z), F32)
                for block in range(blocks):
                    value = jnp.where(ids == block, metric_ref[axis, block], value)
                spacing[axis, y, pl.ds(x, 1), :] = 0.5 * value

    plane = cells_x * cells_z
    rest = parts.shape[0] - 2 * total
    parts[pl.ds(2 * total, rest), :] = jnp.zeros((rest, parts.shape[1]), BF16)
    row = iota((rank, cells_z), 0)
    wanted = jnp.zeros((rank, cells_z), jnp.int32)
    for mode in range(rank):
        wanted = jnp.where(row == mode, cell_ref[mode], wanted)
    for comp in range(3):
        for y in range(rows_y):
            for x in range(width_x):
                base = ((comp * rows_y * spaces + sp * rows_y + y) * cells_x + first_x + x) * cells_z
                hit = jnp.where(wanted == base + iota((rank, cells_z), 1), 1.0, 0.0)
                column = ((comp * rows_y + y) * width_x + x) * cells_z
                parts[pl.ds(2 * total, rank), pl.ds(column, cells_z)] = hit.astype(BF16)

    depth = groups.bit_length() - 1
    turns = []
    for level in range(1, depth):
        nodes = groups >> level + 1
        stacked = []
        for k in range(nodes):
            node = groups - (groups >> level) + k
            plain = rot_ref[node].T
            swapped = jnp.concatenate([plain[rank:], plain[:rank]], axis=0)
            flag = order_ref[node].astype(F32)
            stacked.append(plain * (1.0 - flag) + swapped * flag)
        stacked = stacked[0] if nodes == 1 else jnp.concatenate(stacked, axis=0)
        if nodes > 1:
            shape = (rank, rank * nodes)
            copy_out = (iota(shape, 1) % rank == iota(shape, 0)).astype(F32)
            stacked = exact(stacked, copy_out)
            stacked = jnp.where(
                iota(stacked.shape, 0) // (2 * rank) == iota(stacked.shape, 1) // rank, stacked, 0.0
            )
        turns.append(stacked)

    def split_store(start, column, value):
        high, low = split(value)
        parts[pl.ds(start, 2 * here), pl.ds(column, cells_z)] = low
        parts[pl.ds(total + start, 2 * here), pl.ds(column, cells_z)] = high

    def wait_halo(pair):
        for side in range(2):
            x_copy(side, pair).wait_recv()

        @pl.when(sp > 0)
        def _():
            halo_copy(0, pair).wait_recv()

        @pl.when(sp < spaces - 1)
        def _():
            halo_copy(1, pair).wait_recv()

    def curl(pair):
        pair_groups = (2 * pair, 2 * pair + 1)
        start = pl.multiple_of(pair * 2 * here, 2 * here)
        wait_halo(pair)

        def load(ref, *index):
            both = [ref[(group, *index)].astype(F32) for group in pair_groups]
            return [
                jnp.concatenate([item[y * here:(y + 1) * here] for item in both], axis=0)
                for y in range(rows_y)
            ]

        def load_halo(side, x):
            both = [halo[side, group, x].astype(F32) for group in pair_groups]
            return [jnp.concatenate([item[c * here:(c + 1) * here] for item in both], axis=0) for c in range(2)]

        def along_z(field):
            return pltpu.roll(field, cells_z - 1, 1) - pltpu.roll(field, 1, 1)

        for x in range(width_x):
            u_at = load(recv, 0, x + 1)
            v_at = load(recv, 1, x + 1)
            w_at = load(recv, 2, x + 1)
            v_ends = load(recv, 1, x), load(recv, 1, x + 2)
            w_ends = load(recv, 2, x), load(recv, 2, x + 2)
            below = load_halo(0, x)
            above = load_halo(1, x)
            for y in range(rows_y):
                hx, hy, hz = (spacing[axis, y, pl.ds(x, 1), :] for axis in range(3))
                u_down = u_at[y - 1] if y > 0 else below[0]
                w_down = w_at[y - 1] if y > 0 else below[1]
                u_up = u_at[y + 1] if y < rows_y - 1 else above[0]
                w_up = w_at[y + 1] if y < rows_y - 1 else above[1]
                omega = (
                    hy * (w_up - w_down) - hz * along_z(v_at[y]),
                    hz * along_z(u_at[y]) - hx * (w_ends[1][y] - w_ends[0][y]),
                    hx * (v_ends[1][y] - v_ends[0][y]) - hy * (u_up - u_down),
                )
                for comp in range(3):
                    split_store(start, ((comp * rows_y + y) * width_x + x) * cells_z, omega[comp])

    quarter = half // 2
    near = me // half * quarter
    far = quarter - near

    def take(pair):
        for place in range(2):
            source = 2 * pair + place

            @pl.when(source != me)
            def _():
                for copy in arrivals(source):
                    copy.wait_recv()

        forward(pair)

    def take_near(step, carry):
        take(near + step)
        return carry

    def take_far(step, carry):
        take(far + step)
        curl(near + step)
        return carry

    def curl_far(step, carry):
        curl(far + step)
        return carry

    lax.fori_loop(0, quarter, take_near, 0)
    lax.fori_loop(0, quarter, take_far, 0)
    lax.fori_loop(0, quarter, curl_far, 0)

    both = product(parts[:2 * total], parts[total:], ((1,), (1,)))
    crossed = both[:total, :total].T
    gap = jnp.zeros((total, both.shape[1] - total), F32)
    gram_own[...] = (both[:total] + both[total:] + jnp.concatenate([crossed, gap], axis=1)).reshape(gram_own.shape)

    def copy_a(step):
        to = mate(step)
        return pltpu.make_async_remote_copy(
            gram_own.at[to], gram_space.at[step], sem_a_s.at[step], sem_a_r.at[step],
            device_id={"space": to}, device_id_type=MESH,
        )

    for step in range(1, spaces):
        copy_a(step).start()
    lead_all = lead[...].reshape(total, lead_width)[:, :rank * groups // 2]
    part = gram_own[sp]
    for step in range(1, spaces):
        copy_a(step).wait_recv()
        part = part + gram_space[step]
    gram_snap[0] = part

    def copy_b(step):
        return pltpu.make_async_remote_copy(
            gram_snap.at[0], gram_snap.at[step], sem_b_s.at[step], sem_b_r.at[step],
            device_id={"snap": peer(step)}, device_id_type=MESH,
        )

    def start_b(step, carry):
        copy_b(step).start()
        return carry

    def finish_b(step, carry):
        copy_b(step).wait_recv()
        return carry + gram_snap[step]

    lax.fori_loop(1, groups, start_b, 0)
    gram_all[sp] = lax.fori_loop(1, groups, finish_b, part)

    def copy_c(step, owner):
        return pltpu.make_async_remote_copy(
            gram_all.at[owner], gram_all.at[owner], sem_c_s.at[step], sem_c_r.at[step],
            device_id={"space": mate(step)}, device_id_type=MESH,
        )

    for step in range(1, spaces):
        copy_c(step, sp).start()
    for step in range(1, spaces):
        copy_c(step, lax.rem(sp - step + spaces, spaces)).wait_recv()
    summed = gram_all[...].reshape(total, gram_all.shape[2])

    entries = summed[:, total:total + rank]
    maps = lead_all
    gram = exact(maps.T, exact(summed[:, :total], maps))
    for turn in turns:
        step_map = exact(ortho_factor(gram, rank), turn)
        gram = exact(step_map.T, exact(gram, step_map))
        maps = exact(maps, step_map)
    factor = ortho_factor(gram, rank)
    value = jnp.sum(factor * exact(entries.T, maps), axis=1, keepdims=True)
    norm_sq = jnp.sum(factor * exact(factor, gram), axis=1, keepdims=True)
    cells_all = 3 * rows_y * spaces * plane
    floor = 0.5 * jnp.sqrt(norm_sq / cells_all + 1e-06)
    sign = value / jnp.maximum(jnp.abs(value), floor)
    mix = exact(factor, maps.T)
    mix_high, mix_low = split(mix)
    high = parts[total:2 * total]
    both = product(jnp.concatenate([mix_high, mix_low], axis=0), high)
    out_ref[...] = (both[:rank] + both[rank:] + product(mix_high, parts[:total])) * sign

    def finish(step, carry):
        main_copy(step).wait_send()
        return carry

    lax.fori_loop(1, groups, finish, 0)

    def finish_small(step, carry):
        lead_copy(step).wait_send()
        copy_b(step).wait_send()
        return carry

    lax.fori_loop(1, groups, finish_small, 0)
    for step in range(1, spaces):
        copy_a(step).wait_send()
        copy_c(step, sp).wait_send()

    def finish_halo(pair, carry):
        for side in range(2):
            x_copy(side, pair).wait_send()

        @pl.when(sp < spaces - 1)
        def _():
            halo_copy(0, pair).wait_send()

        @pl.when(sp > 0)
        def _():
            halo_copy(1, pair).wait_send()

        return carry

    lax.fori_loop(0, half, finish_halo, 0)


def padded(size, unit):
    return -(-size // unit) * unit


def local(velocity, block_id, metric, leaf_rot, merge_rot, merge_order, ref_cell):
    here, _, rows_y, cells_x, cells_z = velocity.shape
    rank = leaf_rot.shape[2]
    groups = lax.axis_size("snap")
    spaces = lax.axis_size("space")
    total = groups * here
    width_x = cells_x // groups
    tile_rows = rows_y * here
    cells = 3 * rows_y * width_x * cells_z
    gram_width = padded(total + rank, 128)
    share = total // spaces
    lead_width = padded(rank * groups // 2, 128)
    vmem = pl.BlockSpec(memory_space=pltpu.VMEM)
    dma = pltpu.SemaphoreType.DMA
    modes = pl.pallas_call(
        functools.partial(kernel, (groups, spaces)),
        out_shape=jax.ShapeDtypeStruct((rank, cells), F32),
        in_specs=[pl.BlockSpec(memory_space=pltpu.HBM)] * 7,
        out_specs=vmem,
        scratch_shapes=[
            pltpu.VMEM(velocity.shape, BF16),
            pltpu.VMEM(block_id.shape, jnp.int32),
            pltpu.SMEM(metric.shape[::-1], F32),
            pltpu.VMEM(leaf_rot.shape, F32),
            pltpu.VMEM((merge_rot.shape[0], rank, 2 * rank), F32),
            pltpu.SMEM(merge_order.shape, jnp.int32),
            pltpu.SMEM(ref_cell.shape, jnp.int32),
            pltpu.VMEM((here * 3 * rows_y * cells_x, cells_z), F32),
            pltpu.VMEM((groups, 3, width_x, tile_rows, cells_z), BF16),
            pltpu.VMEM((groups, 3, width_x + 2, tile_rows, cells_z), BF16),
            pltpu.VMEM((2, groups, width_x, 2 * here, cells_z), BF16),
            pltpu.VMEM((2, groups, width_x, 2 * here, cells_z), BF16),
            pltpu.VMEM((groups, here, lead_width), F32),
            pltpu.VMEM((3, rows_y, width_x, cells_z), F32),
            pltpu.VMEM((total + gram_width, cells), BF16),
            pltpu.VMEM((spaces, share, gram_width), F32),
            pltpu.VMEM((spaces, share, gram_width), F32),
            pltpu.VMEM((groups, share, gram_width), F32),
            pltpu.VMEM((spaces, share, gram_width), F32),
        ]
        + [dma((7,))]
        + [dma((groups,))] * 2
        + [dma((2, groups // 2))] * 2
        + [dma((groups,))] * 2
        + [dma((2, groups // 2))] * 2
        + [dma((spaces,))] * 2
        + [dma((groups,))] * 2
        + [dma((spaces,))] * 2,
        compiler_params=pltpu.CompilerParams(
            collective_id=0, has_side_effects=True, vmem_limit_bytes=56 * 1024 * 1024
        ),
    )(velocity, block_id, metric.T, leaf_rot, jnp.swapaxes(merge_rot, 1, 2), merge_order, ref_cell)
    return modes.reshape(rank, 3, rows_y, width_x * cells_z)


def solution(mesh):
    placed = (
        P("snap", None, "space", None, None),
        P("space", None, None),
        P(),
        P("snap", None, None),
        P(),
        P(),
        P(),
    )
    return jax.shard_map(
        local, mesh=mesh, in_specs=placed, out_specs=P(None, None, "space", "snap"), check_vma=False
    )
```

```python
import functools

import jax
import jax.numpy as jnp
from jax import lax
from jax.experimental import pallas as pl
from jax.experimental.pallas import tpu as pltpu
from jax.sharding import PartitionSpec as P

HIGHEST = lax.Precision.HIGHEST
MESH = pl.DeviceIdType.MESH
F32 = jnp.float32
BF16 = jnp.bfloat16


def exact(left, right, dims=((1,), (0,))):
    return lax.dot_general(left, right, (dims, ((), ())), precision=HIGHEST, preferred_element_type=F32)


def product(left, right, dims=((1,), (0,))):
    return lax.dot_general(left, right, (dims, ((), ())), preferred_element_type=F32)


def split(value):
    high = value.astype(BF16)
    return high, (value - high.astype(F32)).astype(BF16)


def iota(shape, dim):
    return lax.broadcasted_iota(jnp.int32, shape, dim)


def ortho_factor(gram, rank):
    size = gram.shape[0]
    eye = iota(gram.shape, 0) == iota(gram.shape, 1)
    same = iota(gram.shape, 0) // rank == iota(gram.shape, 1) // rank
    diagonal = jnp.sum(jnp.where(eye, gram, 0.0), axis=0, keepdims=True)
    node_of = iota((1, size), 1) // rank
    trace = jnp.zeros((1, size), F32)
    for node in range(size // rank):
        own = jnp.where(node_of == node, diagonal, 0.0)
        trace = jnp.where(node_of == node, jnp.sum(own, axis=1, keepdims=True), trace)
    scale = (trace + 1e-06) / rank
    return 1.5 * eye.astype(F32) - jnp.where(same, 0.5 * gram / scale, 0.0)


def kernel(
    dims,
    vel_hbm, block_hbm, metric_hbm, leaf_hbm, rot_hbm, order_hbm, cell_hbm, out_ref,
    vel_ref, block_ref, metric_ref, leaf_ref, rot_ref, order_ref, cell_ref,
    velf, send_u, send_vw, recv_u, recv_vw, stage, halo, lead, spacing, parts,
    gram_own, gram_space, gram_snap, gram_all,
    sem_in, sem_u_s, sem_u_r, sem_vw_s, sem_vw_r, sem_lead_s, sem_lead_r, sem_halo_s, sem_halo_r,
    sem_a_s, sem_a_r, sem_b_s, sem_b_r, sem_c_s, sem_c_r,
):
    groups, spaces = dims
    here, _, rows_y, cells_x, cells_z = vel_ref.shape
    rank = leaf_ref.shape[2]
    blocks = metric_ref.shape[1]
    total = groups * here
    width_x = cells_x // groups
    me = lax.axis_index("snap")
    sp = lax.axis_index("space")
    first_x = me * width_x

    loads = [
        pltpu.make_async_copy(source, place, sem_in.at[index])
        for index, (source, place) in enumerate((
            (vel_hbm, vel_ref), (block_hbm, block_ref), (metric_hbm, metric_ref), (leaf_hbm, leaf_ref),
            (rot_hbm, rot_ref), (order_hbm, order_ref), (cell_hbm, cell_ref),
        ))
    ]
    for load in loads:
        load.start()

    def peer(step):
        return lax.rem(me + step, groups)

    def mate(step):
        return lax.rem(sp + step, spaces)

    barrier = pltpu.get_barrier_semaphore()
    for step in range(1, spaces):
        pl.semaphore_signal(barrier, inc=1, device_id={"space": mate(step)}, device_id_type=MESH)

    def greet(step, carry):
        pl.semaphore_signal(barrier, inc=1, device_id={"snap": peer(step)}, device_id_type=MESH)
        return carry

    lax.fori_loop(1, groups, greet, 0)

    stretch = 3 * rows_y * cells_x

    def widen(snap, carry):
        start = pl.multiple_of(snap * stretch, stretch)
        velf[pl.ds(start, stretch), :] = vel_ref[snap].reshape(stretch, cells_z).astype(F32)
        return carry

    loads[0].wait()
    lax.fori_loop(0, here, widen, 0)

    def tile(comp, x):
        pieces = [
            velf[pl.ds((comp * rows_y + y) * cells_x + x, here, stride=stretch), :]
            for y in range(rows_y)
        ]
        return jnp.concatenate(pieces, axis=0).astype(BF16)

    def regroup(x, carry):
        send_u[x] = tile(0, x)
        send_vw[0, x + 1] = tile(1, x)
        send_vw[1, x + 1] = tile(2, x)
        return carry

    lax.fori_loop(0, cells_x, regroup, 0, unroll=4)
    for comp in range(2):
        send_vw[comp, 0] = send_vw[comp, cells_x]
        send_vw[comp, cells_x + 1] = send_vw[comp, 1]

    pl.semaphore_wait(barrier, groups + spaces - 2)

    def copies(step):
        to = peer(step)
        start = to * width_x
        return (
            pltpu.make_async_remote_copy(
                send_vw.at[:, pl.ds(start, width_x + 2)], recv_vw.at[me],
                sem_vw_s.at[step], sem_vw_r.at[me], device_id={"snap": to}, device_id_type=MESH,
            ),
            pltpu.make_async_remote_copy(
                send_u.at[pl.ds(start, width_x)], recv_u.at[me],
                sem_u_s.at[step], sem_u_r.at[me], device_id={"snap": to}, device_id_type=MESH,
            ),
        )

    def arrivals(source):
        return (
            pltpu.make_async_remote_copy(
                recv_vw.at[source], recv_vw.at[source],
                sem_vw_s.at[0], sem_vw_r.at[source], device_id={"snap": source}, device_id_type=MESH,
            ),
            pltpu.make_async_remote_copy(
                recv_u.at[source], recv_u.at[source],
                sem_u_s.at[0], sem_u_r.at[source], device_id={"snap": source}, device_id_type=MESH,
            ),
            pltpu.make_async_remote_copy(
                lead.at[source], lead.at[source],
                sem_lead_s.at[0], sem_lead_r.at[source], device_id={"snap": source}, device_id_type=MESH,
            ),
        )

    def launch(step, carry):
        for copy in copies(step):
            copy.start()
        return carry

    lax.fori_loop(1, groups, launch, 0)

    for load in loads[1:]:
        load.wait()

    lead_width = lead.shape[2]
    turn = rot_ref[me // 2].T
    pick = (order_ref[me // 2] - me % 2).astype(F32)
    pick = pick * pick
    turn_own = turn[:rank] * (1.0 - pick) + turn[rank:] * pick
    lead_own = exact(leaf_ref[0], turn_own)
    repeat = (iota((rank, lead_width), 1) % rank == iota((rank, lead_width), 0)).astype(F32)
    lead_wide = exact(lead_own, repeat)
    lead[me] = jnp.where(iota(lead_wide.shape, 1) // rank == me // 2, lead_wide, 0.0)

    def lead_copy(step):
        return pltpu.make_async_remote_copy(
            lead.at[me], lead.at[me],
            sem_lead_s.at[step], sem_lead_r.at[me], device_id={"snap": peer(step)}, device_id_type=MESH,
        )

    def launch_lead(step, carry):
        lead_copy(step).start()
        return carry

    lax.fori_loop(1, groups, launch_lead, 0)

    def halo_copy(side, group):
        to = sp + 1 if side == 0 else sp - 1
        return pltpu.make_async_remote_copy(
            stage.at[side, group], halo.at[side, group],
            sem_halo_s.at[side, group], sem_halo_r.at[side, group],
            device_id={"space": to}, device_id_type=MESH,
        )

    def forward(group):
        for x in range(width_x):
            u_here = recv_u[group, x].astype(F32)
            w_here = recv_vw[group, 1, x + 1].astype(F32)
            stage[1, group, x] = jnp.concatenate([u_here[:here], w_here[:here]], axis=0).astype(BF16)
            stage[0, group, x] = jnp.concatenate([u_here[-here:], w_here[-here:]], axis=0).astype(BF16)

        @pl.when(sp < spaces - 1)
        def _():
            halo_copy(0, group).start()

        @pl.when(sp > 0)
        def _():
            halo_copy(1, group).start()

    recv_u[me] = send_u[pl.ds(first_x, width_x)]
    recv_vw[me] = send_vw[:, pl.ds(first_x, width_x + 2)]
    forward(me)

    @pl.when(sp == 0)
    def _():
        halo[0] = jnp.zeros(halo.shape[1:], BF16)

    @pl.when(sp == spaces - 1)
    def _():
        halo[1] = jnp.zeros(halo.shape[1:], BF16)

    for y in range(rows_y):
        for x in range(width_x):
            ids = block_ref[y, pl.ds(first_x + x, 1), :]
            for axis in range(3):
                value = jnp.zeros((1, cells_z), F32)
                for block in range(blocks):
                    value = jnp.where(ids == block, metric_ref[axis, block], value)
                spacing[axis, y, pl.ds(x, 1), :] = 0.5 * value

    plane = cells_x * cells_z
    rest = parts.shape[0] - 2 * total
    parts[pl.ds(2 * total, rest), :] = jnp.zeros((rest, parts.shape[1]), BF16)
    row = iota((rank, cells_z), 0)
    wanted = jnp.zeros((rank, cells_z), jnp.int32)
    for mode in range(rank):
        wanted = jnp.where(row == mode, cell_ref[mode], wanted)
    for comp in range(3):
        for y in range(rows_y):
            for x in range(width_x):
                base = ((comp * rows_y * spaces + sp * rows_y + y) * cells_x + first_x + x) * cells_z
                hit = jnp.where(wanted == base + iota((rank, cells_z), 1), 1.0, 0.0)
                column = ((comp * rows_y + y) * width_x + x) * cells_z
                parts[pl.ds(2 * total, rank), pl.ds(column, cells_z)] = hit.astype(BF16)

    depth = groups.bit_length() - 1
    turns = []
    for level in range(1, depth):
        nodes = groups >> level + 1
        stacked = []
        for k in range(nodes):
            node = groups - (groups >> level) + k
            plain = rot_ref[node].T
            swapped = jnp.concatenate([plain[rank:], plain[:rank]], axis=0)
            flag = order_ref[node].astype(F32)
            stacked.append(plain * (1.0 - flag) + swapped * flag)
        stacked = stacked[0] if nodes == 1 else jnp.concatenate(stacked, axis=0)
        if nodes > 1:
            shape = (rank, rank * nodes)
            copy_out = (iota(shape, 1) % rank == iota(shape, 0)).astype(F32)
            stacked = exact(stacked, copy_out)
            stacked = jnp.where(
                iota(stacked.shape, 0) // (2 * rank) == iota(stacked.shape, 1) // rank, stacked, 0.0
            )
        turns.append(stacked)

    def receive(step, carry):
        source = lax.rem(me - step + groups, groups)
        for copy in arrivals(source):
            copy.wait_recv()
        forward(source)
        return carry

    lax.fori_loop(1, groups, receive, 0)

    def split_store(start, column, value):
        high, low = split(value)
        parts[pl.ds(start, 2 * here), pl.ds(column, cells_z)] = low
        parts[pl.ds(total + start, 2 * here), pl.ds(column, cells_z)] = high

    def wait_halo(group):
        @pl.when(sp > 0)
        def _():
            halo_copy(0, group).wait_recv()

        @pl.when(sp < spaces - 1)
        def _():
            halo_copy(1, group).wait_recv()

    def curl(pair, carry):
        pair_groups = (2 * pair, 2 * pair + 1)
        start = pl.multiple_of(pair * 2 * here, 2 * here)
        for group in pair_groups:
            wait_halo(group)

        def load(ref, *index):
            both = [ref[(group, *index)].astype(F32) for group in pair_groups]
            return [
                jnp.concatenate([item[y * here:(y + 1) * here] for item in both], axis=0)
                for y in range(rows_y)
            ]

        def load_halo(side, x):
            both = [halo[side, group, x].astype(F32) for group in pair_groups]
            return [jnp.concatenate([item[c * here:(c + 1) * here] for item in both], axis=0) for c in range(2)]

        def along_z(field):
            return pltpu.roll(field, cells_z - 1, 1) - pltpu.roll(field, 1, 1)

        for x in range(width_x):
            u_at = load(recv_u, x)
            v_at = load(recv_vw, 0, x + 1)
            w_at = load(recv_vw, 1, x + 1)
            v_ends = load(recv_vw, 0, x), load(recv_vw, 0, x + 2)
            w_ends = load(recv_vw, 1, x), load(recv_vw, 1, x + 2)
            below = load_halo(0, x)
            above = load_halo(1, x)
            for y in range(rows_y):
                hx, hy, hz = (spacing[axis, y, pl.ds(x, 1), :] for axis in range(3))
                u_down = u_at[y - 1] if y > 0 else below[0]
                w_down = w_at[y - 1] if y > 0 else below[1]
                u_up = u_at[y + 1] if y < rows_y - 1 else above[0]
                w_up = w_at[y + 1] if y < rows_y - 1 else above[1]
                omega = (
                    hy * (w_up - w_down) - hz * along_z(v_at[y]),
                    hz * along_z(u_at[y]) - hx * (w_ends[1][y] - w_ends[0][y]),
                    hx * (v_ends[1][y] - v_ends[0][y]) - hy * (u_up - u_down),
                )
                for comp in range(3):
                    split_store(start, ((comp * rows_y + y) * width_x + x) * cells_z, omega[comp])
        return carry

    lax.fori_loop(0, groups // 2, curl, 0)

    both = product(parts[:2 * total], parts[total:], ((1,), (1,)))
    crossed = both[:total, :total].T
    gap = jnp.zeros((total, both.shape[1] - total), F32)
    gram_own[...] = (both[:total] + both[total:] + jnp.concatenate([crossed, gap], axis=1)).reshape(gram_own.shape)

    def copy_a(step):
        to = mate(step)
        return pltpu.make_async_remote_copy(
            gram_own.at[to], gram_space.at[step], sem_a_s.at[step], sem_a_r.at[step],
            device_id={"space": to}, device_id_type=MESH,
        )

    for step in range(1, spaces):
        copy_a(step).start()
    lead_all = lead[...].reshape(total, lead_width)[:, :rank * groups // 2]
    part = gram_own[sp]
    for step in range(1, spaces):
        copy_a(step).wait_recv()
        part = part + gram_space[step]
    gram_snap[0] = part

    def copy_b(step):
        return pltpu.make_async_remote_copy(
            gram_snap.at[0], gram_snap.at[step], sem_b_s.at[step], sem_b_r.at[step],
            device_id={"snap": peer(step)}, device_id_type=MESH,
        )

    def start_b(step, carry):
        copy_b(step).start()
        return carry

    def finish_b(step, carry):
        copy_b(step).wait_recv()
        return carry + gram_snap[step]

    lax.fori_loop(1, groups, start_b, 0)
    gram_all[sp] = lax.fori_loop(1, groups, finish_b, part)

    def copy_c(step, owner):
        return pltpu.make_async_remote_copy(
            gram_all.at[owner], gram_all.at[owner], sem_c_s.at[step], sem_c_r.at[step],
            device_id={"space": mate(step)}, device_id_type=MESH,
        )

    for step in range(1, spaces):
        copy_c(step, sp).start()
    for step in range(1, spaces):
        copy_c(step, lax.rem(sp - step + spaces, spaces)).wait_recv()
    summed = gram_all[...].reshape(total, gram_all.shape[2])

    first = ((0,), (0,))
    entries = summed[:, total:total + rank]
    maps = lead_all
    gram = exact(maps, exact(summed[:, :total], maps), first)
    for turn in turns:
        step_map = exact(ortho_factor(gram, rank), turn)
        gram = exact(step_map, exact(gram, step_map), first)
        maps = exact(maps, step_map)
    factor = ortho_factor(gram, rank)
    value = jnp.sum(factor * exact(entries, maps, first), axis=1, keepdims=True)
    norm_sq = jnp.sum(factor * exact(factor, gram), axis=1, keepdims=True)
    cells_all = 3 * rows_y * spaces * plane
    floor = 0.5 * jnp.sqrt(norm_sq / cells_all + 1e-06)
    sign = value / jnp.maximum(jnp.abs(value), floor)
    mix = exact(factor, maps, ((1,), (1,)))
    mix_high, mix_low = split(mix)
    both = product(jnp.concatenate([mix_high, mix_low], axis=0), parts[total:2 * total])
    out_ref[...] = (both[:rank] + both[rank:] + product(mix_high, parts[:total])) * sign

    def finish(step, carry):
        for copy in copies(step):
            copy.wait_send()
        lead_copy(step).wait_send()
        copy_b(step).wait_send()
        return carry

    lax.fori_loop(1, groups, finish, 0)
    for step in range(1, spaces):
        copy_a(step).wait_send()
        copy_c(step, sp).wait_send()

    def finish_halo(group, carry):
        @pl.when(sp < spaces - 1)
        def _():
            halo_copy(0, group).wait_send()

        @pl.when(sp > 0)
        def _():
            halo_copy(1, group).wait_send()

        return carry

    lax.fori_loop(0, groups, finish_halo, 0)


def padded(size, unit):
    return -(-size // unit) * unit


def local(velocity, block_id, metric, leaf_rot, merge_rot, merge_order, ref_cell):
    here, _, rows_y, cells_x, cells_z = velocity.shape
    rank = leaf_rot.shape[2]
    groups = lax.axis_size("snap")
    spaces = lax.axis_size("space")
    total = groups * here
    width_x = cells_x // groups
    tile_rows = rows_y * here
    cells = 3 * rows_y * width_x * cells_z
    gram_width = padded(total + rank, 128)
    share = total // spaces
    lead_width = padded(rank * groups // 2, 128)
    vmem = pl.BlockSpec(memory_space=pltpu.VMEM)
    dma = pltpu.SemaphoreType.DMA
    modes = pl.pallas_call(
        functools.partial(kernel, (groups, spaces)),
        out_shape=jax.ShapeDtypeStruct((rank, cells), F32),
        in_specs=[pl.BlockSpec(memory_space=pltpu.HBM)] * 7,
        out_specs=vmem,
        scratch_shapes=[
            pltpu.VMEM(velocity.shape, BF16),
            pltpu.VMEM(block_id.shape, jnp.int32),
            pltpu.SMEM(metric.shape[::-1], F32),
            pltpu.VMEM(leaf_rot.shape, F32),
            pltpu.VMEM((merge_rot.shape[0], rank, 2 * rank), F32),
            pltpu.SMEM(merge_order.shape, jnp.int32),
            pltpu.SMEM(ref_cell.shape, jnp.int32),
            pltpu.VMEM((here * 3 * rows_y * cells_x, cells_z), F32),
            pltpu.VMEM((cells_x, tile_rows, cells_z), BF16),
            pltpu.VMEM((2, cells_x + 2, tile_rows, cells_z), BF16),
            pltpu.VMEM((groups, width_x, tile_rows, cells_z), BF16),
            pltpu.VMEM((groups, 2, width_x + 2, tile_rows, cells_z), BF16),
            pltpu.VMEM((2, groups, width_x, 2 * here, cells_z), BF16),
            pltpu.VMEM((2, groups, width_x, 2 * here, cells_z), BF16),
            pltpu.VMEM((groups, here, lead_width), F32),
            pltpu.VMEM((3, rows_y, width_x, cells_z), F32),
            pltpu.VMEM((total + gram_width, cells), BF16),
            pltpu.VMEM((spaces, share, gram_width), F32),
            pltpu.VMEM((spaces, share, gram_width), F32),
            pltpu.VMEM((groups, share, gram_width), F32),
            pltpu.VMEM((spaces, share, gram_width), F32),
        ]
        + [dma((7,))]
        + [dma((groups,))] * 6
        + [dma((2, groups))] * 2
        + [dma((spaces,))] * 2
        + [dma((groups,))] * 2
        + [dma((spaces,))] * 2,
        compiler_params=pltpu.CompilerParams(
            collective_id=0, has_side_effects=True, vmem_limit_bytes=56 * 1024 * 1024
        ),
    )(velocity, block_id, metric.T, leaf_rot, jnp.swapaxes(merge_rot, 1, 2), merge_order, ref_cell)
    return modes.reshape(rank, 3, rows_y, width_x * cells_z)


def solution(mesh):
    placed = (
        P("snap", None, "space", None, None),
        P("space", None, None),
        P(),
        P("snap", None, None),
        P(),
        P(),
        P(),
    )
    return jax.shard_map(
        local, mesh=mesh, in_specs=placed, out_specs=P(None, None, "space", "snap"), check_vma=False
    )
```

```python
import functools

import jax
import jax.numpy as jnp
from jax import lax
from jax.experimental import pallas as pl
from jax.experimental.pallas import tpu as pltpu
from jax.sharding import PartitionSpec as P

HIGHEST = lax.Precision.HIGHEST
MESH = pl.DeviceIdType.MESH
F32 = jnp.float32
BF16 = jnp.bfloat16


def exact(left, right, dims=((1,), (0,))):
    return lax.dot_general(left, right, (dims, ((), ())), precision=HIGHEST, preferred_element_type=F32)


def product(left, right, dims=((1,), (0,))):
    return lax.dot_general(left, right, (dims, ((), ())), preferred_element_type=F32)


def split(value):
    high = value.astype(BF16)
    return high, (value - high.astype(F32)).astype(BF16)


def iota(shape, dim):
    return lax.broadcasted_iota(jnp.int32, shape, dim)


def ortho_factor(gram, rank):
    size = gram.shape[0]
    eye = iota(gram.shape, 0) == iota(gram.shape, 1)
    same = iota(gram.shape, 0) // rank == iota(gram.shape, 1) // rank
    diagonal = jnp.sum(jnp.where(eye, gram, 0.0), axis=0, keepdims=True)
    node_of = iota((1, size), 1) // rank
    trace = jnp.zeros((1, size), F32)
    for node in range(size // rank):
        own = jnp.where(node_of == node, diagonal, 0.0)
        trace = jnp.where(node_of == node, jnp.sum(own, axis=1, keepdims=True), trace)
    scale = (trace + 1e-06) / rank
    return 1.5 * eye.astype(F32) - jnp.where(same, 0.5 * gram / scale, 0.0)


def kernel(
    dims,
    vel_hbm, block_hbm, metric_hbm, leaf_hbm, rot_hbm, order_hbm, cell_hbm, out_ref,
    vel_ref, block_ref, metric_ref, leaf_ref, rot_ref, order_ref, cell_ref,
    velf, send_u, send_vw, recv_u, recv_vw, stage, halo, lead, spacing, parts,
    gram_own, gram_space, gram_snap, gram_all,
    sem_in, sem_u_s, sem_u_r, sem_vw_s, sem_vw_r, sem_lead_s, sem_lead_r, sem_halo_s, sem_halo_r,
    sem_a_s, sem_a_r, sem_b_s, sem_b_r, sem_c_s, sem_c_r,
):
    groups, spaces = dims
    here, _, rows_y, cells_x, cells_z = vel_ref.shape
    rank = leaf_ref.shape[2]
    blocks = metric_ref.shape[1]
    total = groups * here
    width_x = cells_x // groups
    me = lax.axis_index("snap")
    sp = lax.axis_index("space")
    first_x = me * width_x

    loads = [
        pltpu.make_async_copy(source, place, sem_in.at[index])
        for index, (source, place) in enumerate((
            (vel_hbm, vel_ref), (block_hbm, block_ref), (metric_hbm, metric_ref), (leaf_hbm, leaf_ref),
            (rot_hbm, rot_ref), (order_hbm, order_ref), (cell_hbm, cell_ref),
        ))
    ]
    loads[0].start()

    def peer(step):
        return lax.rem(me + step, groups)

    def mate(step):
        return lax.rem(sp + step, spaces)

    barrier = pltpu.get_barrier_semaphore()
    for step in range(1, spaces):
        pl.semaphore_signal(barrier, inc=1, device_id={"space": mate(step)}, device_id_type=MESH)

    def greet(step, carry):
        pl.semaphore_signal(barrier, inc=1, device_id={"snap": peer(step)}, device_id_type=MESH)
        return carry

    lax.fori_loop(1, groups, greet, 0)
    for load in loads[1:]:
        load.start()

    stretch = 3 * rows_y * cells_x

    def widen(snap, carry):
        start = pl.multiple_of(snap * stretch, stretch)
        velf[pl.ds(start, stretch), :] = vel_ref[snap].reshape(stretch, cells_z).astype(F32)
        return carry

    loads[0].wait()
    lax.fori_loop(0, here, widen, 0)

    def tile(comp, x):
        pieces = [
            velf[pl.ds((comp * rows_y + y) * cells_x + x, here, stride=stretch), :]
            for y in range(rows_y)
        ]
        return jnp.concatenate(pieces, axis=0).astype(BF16)

    def regroup(x, carry):
        send_u[x] = tile(0, x)
        send_vw[0, x + 1] = tile(1, x)
        send_vw[1, x + 1] = tile(2, x)
        return carry

    lax.fori_loop(0, cells_x, regroup, 0, unroll=4)
    for comp in range(2):
        send_vw[comp, 0] = send_vw[comp, cells_x]
        send_vw[comp, cells_x + 1] = send_vw[comp, 1]

    pl.semaphore_wait(barrier, groups + spaces - 2)

    def copies(step):
        to = peer(step)
        start = to * width_x
        return (
            pltpu.make_async_remote_copy(
                send_vw.at[:, pl.ds(start, width_x + 2)], recv_vw.at[me],
                sem_vw_s.at[step], sem_vw_r.at[me], device_id={"snap": to}, device_id_type=MESH,
            ),
            pltpu.make_async_remote_copy(
                send_u.at[pl.ds(start, width_x)], recv_u.at[me],
                sem_u_s.at[step], sem_u_r.at[me], device_id={"snap": to}, device_id_type=MESH,
            ),
        )

    def arrivals(source):
        return (
            pltpu.make_async_remote_copy(
                recv_vw.at[source], recv_vw.at[source],
                sem_vw_s.at[0], sem_vw_r.at[source], device_id={"snap": source}, device_id_type=MESH,
            ),
            pltpu.make_async_remote_copy(
                recv_u.at[source], recv_u.at[source],
                sem_u_s.at[0], sem_u_r.at[source], device_id={"snap": source}, device_id_type=MESH,
            ),
            pltpu.make_async_remote_copy(
                lead.at[source], lead.at[source],
                sem_lead_s.at[0], sem_lead_r.at[source], device_id={"snap": source}, device_id_type=MESH,
            ),
        )

    def launch(step, carry):
        for copy in copies(step):
            copy.start()
        return carry

    lax.fori_loop(1, groups, launch, 0)

    for load in loads[1:]:
        load.wait()

    lead_width = lead.shape[2]
    turn = rot_ref[me // 2].T
    pick = (order_ref[me // 2] - me % 2).astype(F32)
    pick = pick * pick
    turn_own = turn[:rank] * (1.0 - pick) + turn[rank:] * pick
    lead_own = exact(leaf_ref[0], turn_own)
    repeat = (iota((rank, lead_width), 1) % rank == iota((rank, lead_width), 0)).astype(F32)
    lead_wide = exact(lead_own, repeat)
    lead[me] = jnp.where(iota(lead_wide.shape, 1) // rank == me // 2, lead_wide, 0.0)

    def lead_copy(step):
        return pltpu.make_async_remote_copy(
            lead.at[me], lead.at[me],
            sem_lead_s.at[step], sem_lead_r.at[me], device_id={"snap": peer(step)}, device_id_type=MESH,
        )

    def launch_lead(step, carry):
        lead_copy(step).start()
        return carry

    lax.fori_loop(1, groups, launch_lead, 0)

    def halo_copy(side, group):
        to = sp + 1 if side == 0 else sp - 1
        return pltpu.make_async_remote_copy(
            stage.at[side, group], halo.at[side, group],
            sem_halo_s.at[side, group], sem_halo_r.at[side, group],
            device_id={"space": to}, device_id_type=MESH,
        )

    def forward(group):
        for x in range(width_x):
            u_here = recv_u[group, x].astype(F32)
            w_here = recv_vw[group, 1, x + 1].astype(F32)
            stage[1, group, x] = jnp.concatenate([u_here[:here], w_here[:here]], axis=0).astype(BF16)
            stage[0, group, x] = jnp.concatenate([u_here[-here:], w_here[-here:]], axis=0).astype(BF16)

        @pl.when(sp < spaces - 1)
        def _():
            halo_copy(0, group).start()

        @pl.when(sp > 0)
        def _():
            halo_copy(1, group).start()

    recv_u[me] = send_u[pl.ds(first_x, width_x)]
    recv_vw[me] = send_vw[:, pl.ds(first_x, width_x + 2)]
    forward(me)

    @pl.when(sp == 0)
    def _():
        halo[0] = jnp.zeros(halo.shape[1:], BF16)

    @pl.when(sp == spaces - 1)
    def _():
        halo[1] = jnp.zeros(halo.shape[1:], BF16)

    for y in range(rows_y):
        for x in range(width_x):
            ids = block_ref[y, pl.ds(first_x + x, 1), :]
            for axis in range(3):
                value = jnp.zeros((1, cells_z), F32)
                for block in range(blocks):
                    value = jnp.where(ids == block, metric_ref[axis, block], value)
                spacing[axis, y, pl.ds(x, 1), :] = 0.5 * value

    plane = cells_x * cells_z
    rest = parts.shape[0] - 2 * total
    parts[pl.ds(2 * total, rest), :] = jnp.zeros((rest, parts.shape[1]), BF16)
    row = iota((rank, cells_z), 0)
    wanted = jnp.zeros((rank, cells_z), jnp.int32)
    for mode in range(rank):
        wanted = jnp.where(row == mode, cell_ref[mode], wanted)
    for comp in range(3):
        for y in range(rows_y):
            for x in range(width_x):
                base = ((comp * rows_y * spaces + sp * rows_y + y) * cells_x + first_x + x) * cells_z
                hit = jnp.where(wanted == base + iota((rank, cells_z), 1), 1.0, 0.0)
                column = ((comp * rows_y + y) * width_x + x) * cells_z
                parts[pl.ds(2 * total, rank), pl.ds(column, cells_z)] = hit.astype(BF16)

    depth = groups.bit_length() - 1
    turns = []
    for level in range(1, depth):
        nodes = groups >> level + 1
        stacked = []
        for k in range(nodes):
            node = groups - (groups >> level) + k
            plain = rot_ref[node].T
            swapped = jnp.concatenate([plain[rank:], plain[:rank]], axis=0)
            flag = order_ref[node].astype(F32)
            stacked.append(plain * (1.0 - flag) + swapped * flag)
        stacked = stacked[0] if nodes == 1 else jnp.concatenate(stacked, axis=0)
        if nodes > 1:
            shape = (rank, rank * nodes)
            copy_out = (iota(shape, 1) % rank == iota(shape, 0)).astype(F32)
            stacked = exact(stacked, copy_out)
            stacked = jnp.where(
                iota(stacked.shape, 0) // (2 * rank) == iota(stacked.shape, 1) // rank, stacked, 0.0
            )
        turns.append(stacked)

    def receive(step, carry):
        source = lax.rem(me - step + groups, groups)
        for copy in arrivals(source):
            copy.wait_recv()
        forward(source)
        return carry

    lax.fori_loop(1, groups, receive, 0)

    def split_store(start, column, value):
        high, low = split(value)
        parts[pl.ds(start, 2 * here), pl.ds(column, cells_z)] = low
        parts[pl.ds(total + start, 2 * here), pl.ds(column, cells_z)] = high

    def wait_halo(group):
        @pl.when(sp > 0)
        def _():
            halo_copy(0, group).wait_recv()

        @pl.when(sp < spaces - 1)
        def _():
            halo_copy(1, group).wait_recv()

    def curl(pair, carry):
        pair_groups = (2 * pair, 2 * pair + 1)
        start = pl.multiple_of(pair * 2 * here, 2 * here)
        for group in pair_groups:
            wait_halo(group)

        def load(ref, *index):
            both = [ref[(group, *index)].astype(F32) for group in pair_groups]
            return [
                jnp.concatenate([item[y * here:(y + 1) * here] for item in both], axis=0)
                for y in range(rows_y)
            ]

        def load_halo(side, x):
            both = [halo[side, group, x].astype(F32) for group in pair_groups]
            return [jnp.concatenate([item[c * here:(c + 1) * here] for item in both], axis=0) for c in range(2)]

        def along_z(field):
            return pltpu.roll(field, cells_z - 1, 1) - pltpu.roll(field, 1, 1)

        for x in range(width_x):
            u_at = load(recv_u, x)
            v_at = load(recv_vw, 0, x + 1)
            w_at = load(recv_vw, 1, x + 1)
            v_ends = load(recv_vw, 0, x), load(recv_vw, 0, x + 2)
            w_ends = load(recv_vw, 1, x), load(recv_vw, 1, x + 2)
            below = load_halo(0, x)
            above = load_halo(1, x)
            for y in range(rows_y):
                hx, hy, hz = (spacing[axis, y, pl.ds(x, 1), :] for axis in range(3))
                u_down = u_at[y - 1] if y > 0 else below[0]
                w_down = w_at[y - 1] if y > 0 else below[1]
                u_up = u_at[y + 1] if y < rows_y - 1 else above[0]
                w_up = w_at[y + 1] if y < rows_y - 1 else above[1]
                omega = (
                    hy * (w_up - w_down) - hz * along_z(v_at[y]),
                    hz * along_z(u_at[y]) - hx * (w_ends[1][y] - w_ends[0][y]),
                    hx * (v_ends[1][y] - v_ends[0][y]) - hy * (u_up - u_down),
                )
                for comp in range(3):
                    split_store(start, ((comp * rows_y + y) * width_x + x) * cells_z, omega[comp])
        return carry

    lax.fori_loop(0, groups // 2, curl, 0)

    both = product(parts[:2 * total], parts[total:], ((1,), (1,)))
    crossed = both[:total, :total].T
    gap = jnp.zeros((total, both.shape[1] - total), F32)
    gram_own[...] = (both[:total] + both[total:] + jnp.concatenate([crossed, gap], axis=1)).reshape(gram_own.shape)

    def copy_a(step):
        to = mate(step)
        return pltpu.make_async_remote_copy(
            gram_own.at[to], gram_space.at[step], sem_a_s.at[step], sem_a_r.at[step],
            device_id={"space": to}, device_id_type=MESH,
        )

    for step in range(1, spaces):
        copy_a(step).start()
    lead_all = lead[...].reshape(total, lead_width)[:, :rank * groups // 2]
    part = gram_own[sp]
    for step in range(1, spaces):
        copy_a(step).wait_recv()
        part = part + gram_space[step]
    gram_snap[0] = part

    def copy_b(step):
        return pltpu.make_async_remote_copy(
            gram_snap.at[0], gram_snap.at[step], sem_b_s.at[step], sem_b_r.at[step],
            device_id={"snap": peer(step)}, device_id_type=MESH,
        )

    def start_b(step, carry):
        copy_b(step).start()
        return carry

    def finish_b(step, carry):
        copy_b(step).wait_recv()
        return carry + gram_snap[step]

    lax.fori_loop(1, groups, start_b, 0)
    gram_all[sp] = lax.fori_loop(1, groups, finish_b, part)

    def copy_c(step, owner):
        return pltpu.make_async_remote_copy(
            gram_all.at[owner], gram_all.at[owner], sem_c_s.at[step], sem_c_r.at[step],
            device_id={"space": mate(step)}, device_id_type=MESH,
        )

    for step in range(1, spaces):
        copy_c(step, sp).start()
    for step in range(1, spaces):
        copy_c(step, lax.rem(sp - step + spaces, spaces)).wait_recv()
    summed = gram_all[...].reshape(total, gram_all.shape[2])

    first = ((0,), (0,))
    entries = summed[:, total:total + rank]
    maps = lead_all
    gram = exact(maps, exact(summed[:, :total], maps), first)
    for turn in turns:
        step_map = exact(ortho_factor(gram, rank), turn)
        gram = exact(step_map, exact(gram, step_map), first)
        maps = exact(maps, step_map)
    factor = ortho_factor(gram, rank)
    value = jnp.sum(factor * exact(entries, maps, first), axis=1, keepdims=True)
    norm_sq = jnp.sum(factor * exact(factor, gram), axis=1, keepdims=True)
    cells_all = 3 * rows_y * spaces * plane
    floor = 0.5 * jnp.sqrt(norm_sq / cells_all + 1e-06)
    sign = value / jnp.maximum(jnp.abs(value), floor)
    mix = exact(factor, maps, ((1,), (1,)))
    mix_high, mix_low = split(mix)
    upper = jnp.concatenate([mix_high, mix_high], axis=1)
    lower = jnp.concatenate([jnp.zeros_like(mix_low), mix_low], axis=1)
    both = product(jnp.concatenate([upper, lower], axis=0), parts[:2 * total])
    modes = (both[:rank] + both[rank:]) * sign
    for comp in range(3):
        for x in range(width_x):
            for y in range(rows_y):
                column = ((comp * rows_y + y) * width_x + x) * cells_z
                row = (comp * width_x + x) * rows_y + y
                out_ref[pl.ds(row, rank, stride=3 * width_x * rows_y), :] = modes[:, column:column + cells_z]

    def finish(step, carry):
        for copy in copies(step):
            copy.wait_send()
        lead_copy(step).wait_send()
        copy_b(step).wait_send()
        return carry

    lax.fori_loop(1, groups, finish, 0)
    for step in range(1, spaces):
        copy_a(step).wait_send()
        copy_c(step, sp).wait_send()

    def finish_halo(group, carry):
        @pl.when(sp < spaces - 1)
        def _():
            halo_copy(0, group).wait_send()

        @pl.when(sp > 0)
        def _():
            halo_copy(1, group).wait_send()

        return carry

    lax.fori_loop(0, groups, finish_halo, 0)


def padded(size, unit):
    return -(-size // unit) * unit


def local(velocity, block_id, metric, leaf_rot, merge_rot, merge_order, ref_cell):
    here, _, rows_y, cells_x, cells_z = velocity.shape
    rank = leaf_rot.shape[2]
    groups = lax.axis_size("snap")
    spaces = lax.axis_size("space")
    total = groups * here
    width_x = cells_x // groups
    tile_rows = rows_y * here
    cells = 3 * rows_y * width_x * cells_z
    gram_width = padded(total + rank, 128)
    share = total // spaces
    lead_width = padded(rank * groups // 2, 128)
    vmem = pl.BlockSpec(memory_space=pltpu.VMEM)
    dma = pltpu.SemaphoreType.DMA
    modes = pl.pallas_call(
        functools.partial(kernel, (groups, spaces)),
        out_shape=jax.ShapeDtypeStruct((rank * cells // cells_z, cells_z), F32),
        in_specs=[pl.BlockSpec(memory_space=pltpu.HBM)] * 7,
        out_specs=vmem,
        scratch_shapes=[
            pltpu.VMEM(velocity.shape, BF16),
            pltpu.VMEM(block_id.shape, jnp.int32),
            pltpu.SMEM(metric.shape[::-1], F32),
            pltpu.VMEM(leaf_rot.shape, F32),
            pltpu.VMEM((merge_rot.shape[0], rank, 2 * rank), F32),
            pltpu.SMEM(merge_order.shape, jnp.int32),
            pltpu.SMEM(ref_cell.shape, jnp.int32),
            pltpu.VMEM((here * 3 * rows_y * cells_x, cells_z), F32),
            pltpu.VMEM((cells_x, tile_rows, cells_z), BF16),
            pltpu.VMEM((2, cells_x + 2, tile_rows, cells_z), BF16),
            pltpu.VMEM((groups, width_x, tile_rows, cells_z), BF16),
            pltpu.VMEM((groups, 2, width_x + 2, tile_rows, cells_z), BF16),
            pltpu.VMEM((2, groups, width_x, 2 * here, cells_z), BF16),
            pltpu.VMEM((2, groups, width_x, 2 * here, cells_z), BF16),
            pltpu.VMEM((groups, here, lead_width), F32),
            pltpu.VMEM((3, rows_y, width_x, cells_z), F32),
            pltpu.VMEM((total + gram_width, cells), BF16),
            pltpu.VMEM((spaces, share, gram_width), F32),
            pltpu.VMEM((spaces, share, gram_width), F32),
            pltpu.VMEM((groups, share, gram_width), F32),
            pltpu.VMEM((spaces, share, gram_width), F32),
        ]
        + [dma((7,))]
        + [dma((groups,))] * 6
        + [dma((2, groups))] * 2
        + [dma((spaces,))] * 2
        + [dma((groups,))] * 2
        + [dma((spaces,))] * 2,
        compiler_params=pltpu.CompilerParams(
            collective_id=0, has_side_effects=True, vmem_limit_bytes=56 * 1024 * 1024
        ),
    )(velocity, block_id, metric.T, leaf_rot, jnp.swapaxes(merge_rot, 1, 2), merge_order, ref_cell)
    modes = modes.reshape(rank, 3, width_x, rows_y, cells_z)
    return jnp.swapaxes(modes, 2, 3).reshape(rank, 3, rows_y, width_x * cells_z)


def solution(mesh):
    placed = (
        P("snap", None, "space", None, None),
        P("space", None, None),
        P(),
        P("snap", None, None),
        P(),
        P(),
        P(),
    )
    return jax.shard_map(
        local, mesh=mesh, in_specs=placed, out_specs=P(None, None, "space", "snap"), check_vma=False
    )
```

```python
import functools

import jax
import jax.numpy as jnp
from jax import lax
from jax.experimental import pallas as pl
from jax.experimental.pallas import tpu as pltpu
from jax.sharding import PartitionSpec as P

HIGHEST = lax.Precision.HIGHEST
MESH = pl.DeviceIdType.MESH
F32 = jnp.float32
BF16 = jnp.bfloat16


def exact(left, right, dims=((1,), (0,))):
    return lax.dot_general(left, right, (dims, ((), ())), precision=HIGHEST, preferred_element_type=F32)


def product(left, right, dims=((1,), (0,))):
    return lax.dot_general(left, right, (dims, ((), ())), preferred_element_type=F32)


def split(value):
    high = value.astype(BF16)
    return high, (value - high.astype(F32)).astype(BF16)


def iota(shape, dim):
    return lax.broadcasted_iota(jnp.int32, shape, dim)


def ortho_factor(gram, rank):
    size = gram.shape[0]
    eye = iota(gram.shape, 0) == iota(gram.shape, 1)
    same = iota(gram.shape, 0) // rank == iota(gram.shape, 1) // rank
    diagonal = jnp.sum(jnp.where(eye, gram, 0.0), axis=0, keepdims=True)
    node_of = iota((1, size), 1) // rank
    trace = jnp.zeros((1, size), F32)
    for node in range(size // rank):
        own = jnp.where(node_of == node, diagonal, 0.0)
        trace = jnp.where(node_of == node, jnp.sum(own, axis=1, keepdims=True), trace)
    scale = (trace + 1e-06) / rank
    return 1.5 * eye.astype(F32) - jnp.where(same, 0.5 * gram / scale, 0.0)


def kernel(
    dims,
    vel_hbm, block_hbm, metric_hbm, leaf_hbm, rot_hbm, order_hbm, cell_hbm, out_ref,
    vel_ref, block_ref, metric_ref, leaf_ref, rot_ref, order_ref, cell_ref,
    velf, send_u, send_vw, recv_u, recv_vw, stage, halo, lead, spacing, parts,
    gram_own, gram_space, gram_snap, gram_all,
    sem_in, sem_u_s, sem_u_r, sem_vw_s, sem_vw_r, sem_lead_s, sem_lead_r, sem_halo_s, sem_halo_r,
    sem_a_s, sem_a_r, sem_b_s, sem_b_r, sem_c_s, sem_c_r,
):
    groups, spaces = dims
    here, _, rows_y, cells_x, cells_z = vel_ref.shape
    rank = leaf_ref.shape[2]
    blocks = metric_ref.shape[1]
    total = groups * here
    width_x = cells_x // groups
    me = lax.axis_index("snap")
    sp = lax.axis_index("space")
    first_x = me * width_x

    loads = [
        pltpu.make_async_copy(source, place, sem_in.at[index])
        for index, (source, place) in enumerate((
            (vel_hbm, vel_ref), (block_hbm, block_ref), (metric_hbm, metric_ref), (leaf_hbm, leaf_ref),
            (rot_hbm, rot_ref), (order_hbm, order_ref), (cell_hbm, cell_ref),
        ))
    ]
    loads[0].start()

    def peer(step):
        return lax.rem(me + step, groups)

    def mate(step):
        return lax.rem(sp + step, spaces)

    barrier = pltpu.get_barrier_semaphore()
    for step in range(1, spaces):
        pl.semaphore_signal(barrier, inc=1, device_id={"space": mate(step)}, device_id_type=MESH)

    def greet(step, carry):
        pl.semaphore_signal(barrier, inc=1, device_id={"snap": peer(step)}, device_id_type=MESH)
        return carry

    lax.fori_loop(1, groups, greet, 0)
    for load in loads[1:]:
        load.start()

    stretch = 3 * rows_y * cells_x

    def widen(snap, carry):
        start = pl.multiple_of(snap * stretch, stretch)
        velf[pl.ds(start, stretch), :] = vel_ref[snap].reshape(stretch, cells_z).astype(F32)
        return carry

    loads[0].wait()
    lax.fori_loop(0, here, widen, 0)

    def tile(comp, x):
        pieces = [
            velf[pl.ds((comp * rows_y + y) * cells_x + x, here, stride=stretch), :]
            for y in range(rows_y)
        ]
        return jnp.concatenate(pieces, axis=0).astype(BF16)

    def regroup(x, carry):
        send_vw[0, x + 1] = tile(1, x)
        send_vw[1, x + 1] = tile(2, x)
        return carry

    lax.fori_loop(0, cells_x, regroup, 0, unroll=4)
    for comp in range(2):
        send_vw[comp, 0] = send_vw[comp, cells_x]
        send_vw[comp, cells_x + 1] = send_vw[comp, 1]

    pl.semaphore_wait(barrier, groups + spaces - 2)

    def regroup_u(x, carry):
        send_u[x] = tile(0, x)
        return carry

    def copies(step):
        to = peer(step)
        start = to * width_x
        return (
            pltpu.make_async_remote_copy(
                send_vw.at[:, pl.ds(start, width_x + 2)], recv_vw.at[me],
                sem_vw_s.at[step], sem_vw_r.at[me], device_id={"snap": to}, device_id_type=MESH,
            ),
            pltpu.make_async_remote_copy(
                send_u.at[pl.ds(start, width_x)], recv_u.at[me],
                sem_u_s.at[step], sem_u_r.at[me], device_id={"snap": to}, device_id_type=MESH,
            ),
        )

    def arrivals(source):
        return (
            pltpu.make_async_remote_copy(
                recv_vw.at[source], recv_vw.at[source],
                sem_vw_s.at[0], sem_vw_r.at[source], device_id={"snap": source}, device_id_type=MESH,
            ),
            pltpu.make_async_remote_copy(
                recv_u.at[source], recv_u.at[source],
                sem_u_s.at[0], sem_u_r.at[source], device_id={"snap": source}, device_id_type=MESH,
            ),
            pltpu.make_async_remote_copy(
                lead.at[source], lead.at[source],
                sem_lead_s.at[0], sem_lead_r.at[source], device_id={"snap": source}, device_id_type=MESH,
            ),
        )

    def launch_vw(step, carry):
        copies(step)[0].start()
        return carry

    def launch_u(step, carry):
        copies(step)[1].start()
        return carry

    lax.fori_loop(1, groups, launch_vw, 0)
    lax.fori_loop(0, cells_x, regroup_u, 0, unroll=4)
    lax.fori_loop(1, groups, launch_u, 0)

    for load in loads[1:]:
        load.wait()

    lead_width = lead.shape[2]
    turn = rot_ref[me // 2].T
    pick = (order_ref[me // 2] - me % 2).astype(F32)
    pick = pick * pick
    turn_own = turn[:rank] * (1.0 - pick) + turn[rank:] * pick
    lead_own = exact(leaf_ref[0], turn_own)
    repeat = (iota((rank, lead_width), 1) % rank == iota((rank, lead_width), 0)).astype(F32)
    lead_wide = exact(lead_own, repeat)
    lead[me] = jnp.where(iota(lead_wide.shape, 1) // rank == me // 2, lead_wide, 0.0)

    def lead_copy(step):
        return pltpu.make_async_remote_copy(
            lead.at[me], lead.at[me],
            sem_lead_s.at[step], sem_lead_r.at[me], device_id={"snap": peer(step)}, device_id_type=MESH,
        )

    def launch_lead(step, carry):
        lead_copy(step).start()
        return carry

    lax.fori_loop(1, groups, launch_lead, 0)

    def halo_copy(side, group):
        to = sp + 1 if side == 0 else sp - 1
        return pltpu.make_async_remote_copy(
            stage.at[side, group], halo.at[side, group],
            sem_halo_s.at[side, group], sem_halo_r.at[side, group],
            device_id={"space": to}, device_id_type=MESH,
        )

    def forward(group):
        for x in range(width_x):
            u_here = recv_u[group, x].astype(F32)
            w_here = recv_vw[group, 1, x + 1].astype(F32)
            stage[1, group, x] = jnp.concatenate([u_here[:here], w_here[:here]], axis=0).astype(BF16)
            stage[0, group, x] = jnp.concatenate([u_here[-here:], w_here[-here:]], axis=0).astype(BF16)

        @pl.when(sp < spaces - 1)
        def _():
            halo_copy(0, group).start()

        @pl.when(sp > 0)
        def _():
            halo_copy(1, group).start()

    recv_u[me] = send_u[pl.ds(first_x, width_x)]
    recv_vw[me] = send_vw[:, pl.ds(first_x, width_x + 2)]
    forward(me)

    @pl.when(sp == 0)
    def _():
        halo[0] = jnp.zeros(halo.shape[1:], BF16)

    @pl.when(sp == spaces - 1)
    def _():
        halo[1] = jnp.zeros(halo.shape[1:], BF16)

    for y in range(rows_y):
        for x in range(width_x):
            ids = block_ref[y, pl.ds(first_x + x, 1), :]
            for axis in range(3):
                value = jnp.zeros((1, cells_z), F32)
                for block in range(blocks):
                    value = jnp.where(ids == block, metric_ref[axis, block], value)
                spacing[axis, y, pl.ds(x, 1), :] = 0.5 * value

    plane = cells_x * cells_z
    rest = parts.shape[0] - 2 * total
    parts[pl.ds(2 * total, rest), :] = jnp.zeros((rest, parts.shape[1]), BF16)
    row = iota((rank, cells_z), 0)
    wanted = jnp.zeros((rank, cells_z), jnp.int32)
    for mode in range(rank):
        wanted = jnp.where(row == mode, cell_ref[mode], wanted)
    for comp in range(3):
        for y in range(rows_y):
            for x in range(width_x):
                base = ((comp * rows_y * spaces + sp * rows_y + y) * cells_x + first_x + x) * cells_z
                hit = jnp.where(wanted == base + iota((rank, cells_z), 1), 1.0, 0.0)
                column = ((comp * rows_y + y) * width_x + x) * cells_z
                parts[pl.ds(2 * total, rank), pl.ds(column, cells_z)] = hit.astype(BF16)

    depth = groups.bit_length() - 1
    turns = []
    for level in range(1, depth):
        nodes = groups >> level + 1
        stacked = []
        for k in range(nodes):
            node = groups - (groups >> level) + k
            plain = rot_ref[node].T
            swapped = jnp.concatenate([plain[rank:], plain[:rank]], axis=0)
            flag = order_ref[node].astype(F32)
            stacked.append(plain * (1.0 - flag) + swapped * flag)
        stacked = stacked[0] if nodes == 1 else jnp.concatenate(stacked, axis=0)
        if nodes > 1:
            shape = (rank, rank * nodes)
            copy_out = (iota(shape, 1) % rank == iota(shape, 0)).astype(F32)
            stacked = exact(stacked, copy_out)
            stacked = jnp.where(
                iota(stacked.shape, 0) // (2 * rank) == iota(stacked.shape, 1) // rank, stacked, 0.0
            )
        turns.append(stacked)

    def receive(step, carry):
        source = lax.rem(me - step + groups, groups)
        for copy in arrivals(source):
            copy.wait_recv()
        forward(source)
        return carry

    lax.fori_loop(1, groups, receive, 0)

    def split_store(start, column, value):
        high, low = split(value)
        parts[pl.ds(start, 2 * here), pl.ds(column, cells_z)] = low
        parts[pl.ds(total + start, 2 * here), pl.ds(column, cells_z)] = high

    def wait_halo(group):
        @pl.when(sp > 0)
        def _():
            halo_copy(0, group).wait_recv()

        @pl.when(sp < spaces - 1)
        def _():
            halo_copy(1, group).wait_recv()

    def curl(pair, carry):
        pair_groups = (2 * pair, 2 * pair + 1)
        start = pl.multiple_of(pair * 2 * here, 2 * here)
        for group in pair_groups:
            wait_halo(group)

        def load(ref, *index):
            both = [ref[(group, *index)].astype(F32) for group in pair_groups]
            return [
                jnp.concatenate([item[y * here:(y + 1) * here] for item in both], axis=0)
                for y in range(rows_y)
            ]

        def load_halo(side, x):
            both = [halo[side, group, x].astype(F32) for group in pair_groups]
            return [jnp.concatenate([item[c * here:(c + 1) * here] for item in both], axis=0) for c in range(2)]

        def along_z(field):
            return pltpu.roll(field, cells_z - 1, 1) - pltpu.roll(field, 1, 1)

        for x in range(width_x):
            u_at = load(recv_u, x)
            v_at = load(recv_vw, 0, x + 1)
            w_at = load(recv_vw, 1, x + 1)
            v_ends = load(recv_vw, 0, x), load(recv_vw, 0, x + 2)
            w_ends = load(recv_vw, 1, x), load(recv_vw, 1, x + 2)
            below = load_halo(0, x)
            above = load_halo(1, x)
            for y in range(rows_y):
                hx, hy, hz = (spacing[axis, y, pl.ds(x, 1), :] for axis in range(3))
                u_down = u_at[y - 1] if y > 0 else below[0]
                w_down = w_at[y - 1] if y > 0 else below[1]
                u_up = u_at[y + 1] if y < rows_y - 1 else above[0]
                w_up = w_at[y + 1] if y < rows_y - 1 else above[1]
                omega = (
                    hy * (w_up - w_down) - hz * along_z(v_at[y]),
                    hz * along_z(u_at[y]) - hx * (w_ends[1][y] - w_ends[0][y]),
                    hx * (v_ends[1][y] - v_ends[0][y]) - hy * (u_up - u_down),
                )
                for comp in range(3):
                    split_store(start, ((comp * rows_y + y) * width_x + x) * cells_z, omega[comp])
        return carry

    lax.fori_loop(0, groups // 2, curl, 0)

    both = product(parts[:2 * total], parts[total:], ((1,), (1,)))
    crossed = both[:total, :total].T
    gap = jnp.zeros((total, both.shape[1] - total), F32)
    gram_own[...] = (both[:total] + both[total:] + jnp.concatenate([crossed, gap], axis=1)).reshape(gram_own.shape)

    def copy_a(step):
        to = mate(step)
        return pltpu.make_async_remote_copy(
            gram_own.at[to], gram_space.at[step], sem_a_s.at[step], sem_a_r.at[step],
            device_id={"space": to}, device_id_type=MESH,
        )

    for step in range(1, spaces):
        copy_a(step).start()
    lead_all = lead[...].reshape(total, lead_width)[:, :rank * groups // 2]
    part = gram_own[sp]
    for step in range(1, spaces):
        copy_a(step).wait_recv()
        part = part + gram_space[step]
    gram_snap[0] = part

    def copy_b(step):
        return pltpu.make_async_remote_copy(
            gram_snap.at[0], gram_snap.at[step], sem_b_s.at[step], sem_b_r.at[step],
            device_id={"snap": peer(step)}, device_id_type=MESH,
        )

    def start_b(step, carry):
        copy_b(step).start()
        return carry

    def finish_b(step, carry):
        copy_b(step).wait_recv()
        return carry + gram_snap[step]

    lax.fori_loop(1, groups, start_b, 0)
    gram_all[sp] = lax.fori_loop(1, groups, finish_b, part)

    def copy_c(step, owner):
        return pltpu.make_async_remote_copy(
            gram_all.at[owner], gram_all.at[owner], sem_c_s.at[step], sem_c_r.at[step],
            device_id={"space": mate(step)}, device_id_type=MESH,
        )

    for step in range(1, spaces):
        copy_c(step, sp).start()
    for step in range(1, spaces):
        copy_c(step, lax.rem(sp - step + spaces, spaces)).wait_recv()
    summed = gram_all[...].reshape(total, gram_all.shape[2])

    first = ((0,), (0,))
    entries = summed[:, total:total + rank]
    maps = lead_all
    gram = exact(maps, exact(summed[:, :total], maps), first)
    for turn in turns:
        step_map = exact(ortho_factor(gram, rank), turn)
        gram = exact(step_map, exact(gram, step_map), first)
        maps = exact(maps, step_map)
    factor = ortho_factor(gram, rank)
    value = jnp.sum(factor * exact(entries, maps, first), axis=1, keepdims=True)
    norm_sq = jnp.sum(factor * exact(factor, gram), axis=1, keepdims=True)
    cells_all = 3 * rows_y * spaces * plane
    floor = 0.5 * jnp.sqrt(norm_sq / cells_all + 1e-06)
    sign = value / jnp.maximum(jnp.abs(value), floor)
    mix = exact(factor, maps, ((1,), (1,)))
    mix_high, mix_low = split(mix)
    upper = jnp.concatenate([mix_high, mix_high], axis=1)
    lower = jnp.concatenate([jnp.zeros_like(mix_low), mix_low], axis=1)
    both = product(jnp.concatenate([upper, lower], axis=0), parts[:2 * total])
    modes = (both[:rank] + both[rank:]) * sign
    for comp in range(3):
        for x in range(width_x):
            for y in range(rows_y):
                column = ((comp * rows_y + y) * width_x + x) * cells_z
                row = (comp * width_x + x) * rows_y + y
                out_ref[pl.ds(row, rank, stride=3 * width_x * rows_y), :] = modes[:, column:column + cells_z]

    def finish(step, carry):
        for copy in copies(step):
            copy.wait_send()
        lead_copy(step).wait_send()
        copy_b(step).wait_send()
        return carry

    lax.fori_loop(1, groups, finish, 0)
    for step in range(1, spaces):
        copy_a(step).wait_send()
        copy_c(step, sp).wait_send()

    def finish_halo(group, carry):
        @pl.when(sp < spaces - 1)
        def _():
            halo_copy(0, group).wait_send()

        @pl.when(sp > 0)
        def _():
            halo_copy(1, group).wait_send()

        return carry

    lax.fori_loop(0, groups, finish_halo, 0)


def padded(size, unit):
    return -(-size // unit) * unit


def local(velocity, block_id, metric, leaf_rot, merge_rot, merge_order, ref_cell):
    here, _, rows_y, cells_x, cells_z = velocity.shape
    rank = leaf_rot.shape[2]
    groups = lax.axis_size("snap")
    spaces = lax.axis_size("space")
    total = groups * here
    width_x = cells_x // groups
    tile_rows = rows_y * here
    cells = 3 * rows_y * width_x * cells_z
    gram_width = padded(total + rank, 128)
    share = total // spaces
    lead_width = padded(rank * groups // 2, 128)
    vmem = pl.BlockSpec(memory_space=pltpu.VMEM)
    dma = pltpu.SemaphoreType.DMA
    modes = pl.pallas_call(
        functools.partial(kernel, (groups, spaces)),
        out_shape=jax.ShapeDtypeStruct((rank * cells // cells_z, cells_z), F32),
        in_specs=[pl.BlockSpec(memory_space=pltpu.HBM)] * 7,
        out_specs=vmem,
        scratch_shapes=[
            pltpu.VMEM(velocity.shape, BF16),
            pltpu.VMEM(block_id.shape, jnp.int32),
            pltpu.SMEM(metric.shape[::-1], F32),
            pltpu.VMEM(leaf_rot.shape, F32),
            pltpu.VMEM((merge_rot.shape[0], rank, 2 * rank), F32),
            pltpu.SMEM(merge_order.shape, jnp.int32),
            pltpu.SMEM(ref_cell.shape, jnp.int32),
            pltpu.VMEM((here * 3 * rows_y * cells_x, cells_z), F32),
            pltpu.VMEM((cells_x, tile_rows, cells_z), BF16),
            pltpu.VMEM((2, cells_x + 2, tile_rows, cells_z), BF16),
            pltpu.VMEM((groups, width_x, tile_rows, cells_z), BF16),
            pltpu.VMEM((groups, 2, width_x + 2, tile_rows, cells_z), BF16),
            pltpu.VMEM((2, groups, width_x, 2 * here, cells_z), BF16),
            pltpu.VMEM((2, groups, width_x, 2 * here, cells_z), BF16),
            pltpu.VMEM((groups, here, lead_width), F32),
            pltpu.VMEM((3, rows_y, width_x, cells_z), F32),
            pltpu.VMEM((total + gram_width, cells), BF16),
            pltpu.VMEM((spaces, share, gram_width), F32),
            pltpu.VMEM((spaces, share, gram_width), F32),
            pltpu.VMEM((groups, share, gram_width), F32),
            pltpu.VMEM((spaces, share, gram_width), F32),
        ]
        + [dma((7,))]
        + [dma((groups,))] * 6
        + [dma((2, groups))] * 2
        + [dma((spaces,))] * 2
        + [dma((groups,))] * 2
        + [dma((spaces,))] * 2,
        compiler_params=pltpu.CompilerParams(
            collective_id=0, has_side_effects=True, vmem_limit_bytes=56 * 1024 * 1024
        ),
    )(velocity, block_id, metric.T, leaf_rot, jnp.swapaxes(merge_rot, 1, 2), merge_order, ref_cell)
    modes = modes.reshape(rank, 3, width_x, rows_y, cells_z)
    return jnp.swapaxes(modes, 2, 3).reshape(rank, 3, rows_y, width_x * cells_z)


def solution(mesh):
    placed = (
        P("snap", None, "space", None, None),
        P("space", None, None),
        P(),
        P("snap", None, None),
        P(),
        P(),
        P(),
    )
    return jax.shard_map(
        local, mesh=mesh, in_specs=placed, out_specs=P(None, None, "space", "snap"), check_vma=False
    )
```

```python
import functools

import jax
import jax.numpy as jnp
from jax import lax
from jax.experimental import pallas as pl
from jax.experimental.pallas import tpu as pltpu
from jax.sharding import PartitionSpec as P

HIGHEST = lax.Precision.HIGHEST
MESH = pl.DeviceIdType.MESH
F32 = jnp.float32
BF16 = jnp.bfloat16


def exact(left, right, dims=((1,), (0,))):
    return lax.dot_general(left, right, (dims, ((), ())), precision=HIGHEST, preferred_element_type=F32)


def product(left, right, dims=((1,), (0,))):
    return lax.dot_general(left, right, (dims, ((), ())), preferred_element_type=F32)


def split(value):
    high = value.astype(BF16)
    return high, (value - high.astype(F32)).astype(BF16)


def iota(shape, dim):
    return lax.broadcasted_iota(jnp.int32, shape, dim)


def ortho_factor(gram, rank):
    size = gram.shape[0]
    eye = iota(gram.shape, 0) == iota(gram.shape, 1)
    same = iota(gram.shape, 0) // rank == iota(gram.shape, 1) // rank
    diagonal = jnp.sum(jnp.where(eye, gram, 0.0), axis=0, keepdims=True)
    node_of = iota((1, size), 1) // rank
    trace = jnp.zeros((1, size), F32)
    for node in range(size // rank):
        own = jnp.where(node_of == node, diagonal, 0.0)
        trace = jnp.where(node_of == node, jnp.sum(own, axis=1, keepdims=True), trace)
    scale = (trace + 1e-06) / rank
    return 1.5 * eye.astype(F32) - jnp.where(same, 0.5 * gram / scale, 0.0)


def kernel(
    dims,
    vel_hbm, block_hbm, metric_hbm, leaf_hbm, rot_hbm, order_hbm, cell_hbm, out_ref,
    vel_ref, block_ref, metric_ref, leaf_ref, rot_ref, order_ref, cell_ref,
    velf, send_u, send_vw, recv_u, recv_vw, stage, halo, lead, spacing, parts,
    gram_own, gram_space, gram_snap, gram_all,
    sem_in, sem_u_s, sem_u_r, sem_vw_s, sem_vw_r, sem_lead_s, sem_lead_r, sem_halo_s, sem_halo_r,
    sem_a_s, sem_a_r, sem_b_s, sem_b_r, sem_c_s, sem_c_r,
):
    groups, spaces = dims
    here, _, rows_y, cells_x, cells_z = vel_ref.shape
    rank = leaf_ref.shape[2]
    blocks = metric_ref.shape[1]
    total = groups * here
    width_x = cells_x // groups
    me = lax.axis_index("snap")
    sp = lax.axis_index("space")
    first_x = me * width_x

    loads = [
        pltpu.make_async_copy(source, place, sem_in.at[index])
        for index, (source, place) in enumerate((
            (vel_hbm, vel_ref), (block_hbm, block_ref), (metric_hbm, metric_ref), (leaf_hbm, leaf_ref),
            (rot_hbm, rot_ref), (order_hbm, order_ref), (cell_hbm, cell_ref),
        ))
    ]
    loads[0].start()

    def peer(step):
        return lax.rem(me + step, groups)

    def mate(step):
        return lax.rem(sp + step, spaces)

    barrier = pltpu.get_barrier_semaphore()
    for step in range(1, spaces):
        pl.semaphore_signal(barrier, inc=1, device_id={"space": mate(step)}, device_id_type=MESH)

    def greet(step, carry):
        pl.semaphore_signal(barrier, inc=1, device_id={"snap": peer(step)}, device_id_type=MESH)
        return carry

    lax.fori_loop(1, groups, greet, 0)
    for load in loads[1:]:
        load.start()

    stretch = 3 * rows_y * cells_x

    def widen(snap, carry):
        start = pl.multiple_of(snap * stretch, stretch)
        velf[pl.ds(start, stretch), :] = vel_ref[snap].reshape(stretch, cells_z).astype(F32)
        return carry

    loads[0].wait()
    lax.fori_loop(0, here, widen, 0, unroll=2)

    def tile(comp, x):
        pieces = [
            velf[pl.ds((comp * rows_y + y) * cells_x + x, here, stride=stretch), :]
            for y in range(rows_y)
        ]
        return jnp.concatenate(pieces, axis=0).astype(BF16)

    def regroup(x, carry):
        send_u[x] = tile(0, x)
        send_vw[0, x + 1] = tile(1, x)
        send_vw[1, x + 1] = tile(2, x)
        return carry

    lax.fori_loop(0, cells_x, regroup, 0, unroll=8)
    for comp in range(2):
        send_vw[comp, 0] = send_vw[comp, cells_x]
        send_vw[comp, cells_x + 1] = send_vw[comp, 1]

    pl.semaphore_wait(barrier, groups + spaces - 2)

    def copies(step):
        to = peer(step)
        start = to * width_x
        return (
            pltpu.make_async_remote_copy(
                send_vw.at[:, pl.ds(start, width_x + 2)], recv_vw.at[me],
                sem_vw_s.at[step], sem_vw_r.at[me], device_id={"snap": to}, device_id_type=MESH,
            ),
            pltpu.make_async_remote_copy(
                send_u.at[pl.ds(start, width_x)], recv_u.at[me],
                sem_u_s.at[step], sem_u_r.at[me], device_id={"snap": to}, device_id_type=MESH,
            ),
        )

    def arrivals(source):
        return (
            pltpu.make_async_remote_copy(
                recv_vw.at[source], recv_vw.at[source],
                sem_vw_s.at[0], sem_vw_r.at[source], device_id={"snap": source}, device_id_type=MESH,
            ),
            pltpu.make_async_remote_copy(
                recv_u.at[source], recv_u.at[source],
                sem_u_s.at[0], sem_u_r.at[source], device_id={"snap": source}, device_id_type=MESH,
            ),
            pltpu.make_async_remote_copy(
                lead.at[source], lead.at[source],
                sem_lead_s.at[0], sem_lead_r.at[source], device_id={"snap": source}, device_id_type=MESH,
            ),
        )

    def launch(step, carry):
        for copy in copies(step):
            copy.start()
        return carry

    lax.fori_loop(1, groups, launch, 0)

    for load in loads[1:]:
        load.wait()

    lead_width = lead.shape[2]
    turn = rot_ref[me // 2].T
    pick = (order_ref[me // 2] - me % 2).astype(F32)
    pick = pick * pick
    turn_own = turn[:rank] * (1.0 - pick) + turn[rank:] * pick
    lead_own = exact(leaf_ref[0], turn_own)
    repeat = (iota((rank, lead_width), 1) % rank == iota((rank, lead_width), 0)).astype(F32)
    lead_wide = exact(lead_own, repeat)
    lead[me] = jnp.where(iota(lead_wide.shape, 1) // rank == me // 2, lead_wide, 0.0)

    def lead_copy(step):
        return pltpu.make_async_remote_copy(
            lead.at[me], lead.at[me],
            sem_lead_s.at[step], sem_lead_r.at[me], device_id={"snap": peer(step)}, device_id_type=MESH,
        )

    def launch_lead(step, carry):
        lead_copy(step).start()
        return carry

    lax.fori_loop(1, groups, launch_lead, 0)

    def halo_copy(side, group):
        to = sp + 1 if side == 0 else sp - 1
        return pltpu.make_async_remote_copy(
            stage.at[side, group], halo.at[side, group],
            sem_halo_s.at[side, group], sem_halo_r.at[side, group],
            device_id={"space": to}, device_id_type=MESH,
        )

    def forward(group):
        for x in range(width_x):
            u_here = recv_u[group, x].astype(F32)
            w_here = recv_vw[group, 1, x + 1].astype(F32)
            stage[1, group, x] = jnp.concatenate([u_here[:here], w_here[:here]], axis=0).astype(BF16)
            stage[0, group, x] = jnp.concatenate([u_here[-here:], w_here[-here:]], axis=0).astype(BF16)

        @pl.when(sp < spaces - 1)
        def _():
            halo_copy(0, group).start()

        @pl.when(sp > 0)
        def _():
            halo_copy(1, group).start()

    recv_u[me] = send_u[pl.ds(first_x, width_x)]
    recv_vw[me] = send_vw[:, pl.ds(first_x, width_x + 2)]
    forward(me)

    @pl.when(sp == 0)
    def _():
        halo[0] = jnp.zeros(halo.shape[1:], BF16)

    @pl.when(sp == spaces - 1)
    def _():
        halo[1] = jnp.zeros(halo.shape[1:], BF16)

    for y in range(rows_y):
        for x in range(width_x):
            ids = block_ref[y, pl.ds(first_x + x, 1), :]
            for axis in range(3):
                value = jnp.zeros((1, cells_z), F32)
                for block in range(blocks):
                    value = jnp.where(ids == block, metric_ref[axis, block], value)
                spacing[axis, y, pl.ds(x, 1), :] = 0.5 * value

    plane = cells_x * cells_z
    rest = parts.shape[0] - 2 * total
    parts[pl.ds(2 * total, rest), :] = jnp.zeros((rest, parts.shape[1]), BF16)
    row = iota((rank, cells_z), 0)
    wanted = jnp.zeros((rank, cells_z), jnp.int32)
    for mode in range(rank):
        wanted = jnp.where(row == mode, cell_ref[mode], wanted)
    for comp in range(3):
        for y in range(rows_y):
            for x in range(width_x):
                base = ((comp * rows_y * spaces + sp * rows_y + y) * cells_x + first_x + x) * cells_z
                hit = jnp.where(wanted == base + iota((rank, cells_z), 1), 1.0, 0.0)
                column = ((comp * rows_y + y) * width_x + x) * cells_z
                parts[pl.ds(2 * total, rank), pl.ds(column, cells_z)] = hit.astype(BF16)

    depth = groups.bit_length() - 1
    turns = []
    for level in range(1, depth):
        nodes = groups >> level + 1
        stacked = []
        for k in range(nodes):
            node = groups - (groups >> level) + k
            plain = rot_ref[node].T
            swapped = jnp.concatenate([plain[rank:], plain[:rank]], axis=0)
            flag = order_ref[node].astype(F32)
            stacked.append(plain * (1.0 - flag) + swapped * flag)
        stacked = stacked[0] if nodes == 1 else jnp.concatenate(stacked, axis=0)
        if nodes > 1:
            shape = (rank, rank * nodes)
            copy_out = (iota(shape, 1) % rank == iota(shape, 0)).astype(F32)
            stacked = exact(stacked, copy_out)
            stacked = jnp.where(
                iota(stacked.shape, 0) // (2 * rank) == iota(stacked.shape, 1) // rank, stacked, 0.0
            )
        turns.append(stacked)

    def receive(step, carry):
        source = lax.rem(me - step + groups, groups)
        for copy in arrivals(source):
            copy.wait_recv()
        forward(source)
        return carry

    lax.fori_loop(1, groups, receive, 0)

    def split_store(start, column, value):
        high, low = split(value)
        parts[pl.ds(start, 2 * here), pl.ds(column, cells_z)] = low
        parts[pl.ds(total + start, 2 * here), pl.ds(column, cells_z)] = high

    def wait_halo(group):
        @pl.when(sp > 0)
        def _():
            halo_copy(0, group).wait_recv()

        @pl.when(sp < spaces - 1)
        def _():
            halo_copy(1, group).wait_recv()

    def curl(pair, carry):
        pair_groups = (2 * pair, 2 * pair + 1)
        start = pl.multiple_of(pair * 2 * here, 2 * here)
        for group in pair_groups:
            wait_halo(group)

        def load(ref, *index):
            both = [ref[(group, *index)].astype(F32) for group in pair_groups]
            return [
                jnp.concatenate([item[y * here:(y + 1) * here] for item in both], axis=0)
                for y in range(rows_y)
            ]

        def load_halo(side, x):
            both = [halo[side, group, x].astype(F32) for group in pair_groups]
            return [jnp.concatenate([item[c * here:(c + 1) * here] for item in both], axis=0) for c in range(2)]

        def along_z(field):
            return pltpu.roll(field, cells_z - 1, 1) - pltpu.roll(field, 1, 1)

        for x in range(width_x):
            u_at = load(recv_u, x)
            v_at = load(recv_vw, 0, x + 1)
            w_at = load(recv_vw, 1, x + 1)
            v_ends = load(recv_vw, 0, x), load(recv_vw, 0, x + 2)
            w_ends = load(recv_vw, 1, x), load(recv_vw, 1, x + 2)
            below = load_halo(0, x)
            above = load_halo(1, x)
            for y in range(rows_y):
                hx, hy, hz = (spacing[axis, y, pl.ds(x, 1), :] for axis in range(3))
                u_down = u_at[y - 1] if y > 0 else below[0]
                w_down = w_at[y - 1] if y > 0 else below[1]
                u_up = u_at[y + 1] if y < rows_y - 1 else above[0]
                w_up = w_at[y + 1] if y < rows_y - 1 else above[1]
                omega = (
                    hy * (w_up - w_down) - hz * along_z(v_at[y]),
                    hz * along_z(u_at[y]) - hx * (w_ends[1][y] - w_ends[0][y]),
                    hx * (v_ends[1][y] - v_ends[0][y]) - hy * (u_up - u_down),
                )
                for comp in range(3):
                    split_store(start, ((comp * rows_y + y) * width_x + x) * cells_z, omega[comp])
        return carry

    lax.fori_loop(0, groups // 2, curl, 0)

    both = product(parts[:2 * total], parts[total:], ((1,), (1,)))
    crossed = both[:total, :total].T
    gap = jnp.zeros((total, both.shape[1] - total), F32)
    gram_own[...] = (both[:total] + both[total:] + jnp.concatenate([crossed, gap], axis=1)).reshape(gram_own.shape)

    def copy_a(step):
        to = mate(step)
        return pltpu.make_async_remote_copy(
            gram_own.at[to], gram_space.at[step], sem_a_s.at[step], sem_a_r.at[step],
            device_id={"space": to}, device_id_type=MESH,
        )

    for step in range(1, spaces):
        copy_a(step).start()
    lead_all = lead[...].reshape(total, lead_width)[:, :rank * groups // 2]
    part = gram_own[sp]
    for step in range(1, spaces):
        copy_a(step).wait_recv()
        part = part + gram_space[step]
    gram_snap[0] = part

    def copy_b(step):
        return pltpu.make_async_remote_copy(
            gram_snap.at[0], gram_snap.at[step], sem_b_s.at[step], sem_b_r.at[step],
            device_id={"snap": peer(step)}, device_id_type=MESH,
        )

    def start_b(step, carry):
        copy_b(step).start()
        return carry

    def finish_b(step, carry):
        copy_b(step).wait_recv()
        return carry + gram_snap[step]

    lax.fori_loop(1, groups, start_b, 0)
    gram_all[sp] = lax.fori_loop(1, groups, finish_b, part)

    def copy_c(step, owner):
        return pltpu.make_async_remote_copy(
            gram_all.at[owner], gram_all.at[owner], sem_c_s.at[step], sem_c_r.at[step],
            device_id={"space": mate(step)}, device_id_type=MESH,
        )

    for step in range(1, spaces):
        copy_c(step, sp).start()
    for step in range(1, spaces):
        copy_c(step, lax.rem(sp - step + spaces, spaces)).wait_recv()
    summed = gram_all[...].reshape(total, gram_all.shape[2])

    first = ((0,), (0,))
    entries = summed[:, total:total + rank]
    maps = lead_all
    gram = exact(maps, exact(summed[:, :total], maps), first)
    for turn in turns:
        step_map = exact(ortho_factor(gram, rank), turn)
        gram = exact(step_map, exact(gram, step_map), first)
        maps = exact(maps, step_map)
    factor = ortho_factor(gram, rank)
    value = jnp.sum(factor * exact(entries, maps, first), axis=1, keepdims=True)
    norm_sq = jnp.sum(factor * exact(factor, gram), axis=1, keepdims=True)
    cells_all = 3 * rows_y * spaces * plane
    floor = 0.5 * jnp.sqrt(norm_sq / cells_all + 1e-06)
    sign = value / jnp.maximum(jnp.abs(value), floor)
    mix = exact(factor, maps, ((1,), (1,)))
    mix_high, mix_low = split(mix)
    upper = jnp.concatenate([mix_high, mix_high], axis=1)
    lower = jnp.concatenate([jnp.zeros_like(mix_low), mix_low], axis=1)
    both = product(jnp.concatenate([upper, lower], axis=0), parts[:2 * total])
    modes = (both[:rank] + both[rank:]) * sign
    for comp in range(3):
        for x in range(width_x):
            for y in range(rows_y):
                column = ((comp * rows_y + y) * width_x + x) * cells_z
                row = (comp * width_x + x) * rows_y + y
                out_ref[pl.ds(row, rank, stride=3 * width_x * rows_y), :] = modes[:, column:column + cells_z]

    def finish(step, carry):
        for copy in copies(step):
            copy.wait_send()
        lead_copy(step).wait_send()
        copy_b(step).wait_send()
        return carry

    lax.fori_loop(1, groups, finish, 0)
    for step in range(1, spaces):
        copy_a(step).wait_send()
        copy_c(step, sp).wait_send()

    def finish_halo(group, carry):
        @pl.when(sp < spaces - 1)
        def _():
            halo_copy(0, group).wait_send()

        @pl.when(sp > 0)
        def _():
            halo_copy(1, group).wait_send()

        return carry

    lax.fori_loop(0, groups, finish_halo, 0)


def padded(size, unit):
    return -(-size // unit) * unit


def local(velocity, block_id, metric, leaf_rot, merge_rot, merge_order, ref_cell):
    here, _, rows_y, cells_x, cells_z = velocity.shape
    rank = leaf_rot.shape[2]
    groups = lax.axis_size("snap")
    spaces = lax.axis_size("space")
    total = groups * here
    width_x = cells_x // groups
    tile_rows = rows_y * here
    cells = 3 * rows_y * width_x * cells_z
    gram_width = padded(total + rank, 128)
    share = total // spaces
    lead_width = padded(rank * groups // 2, 128)
    vmem = pl.BlockSpec(memory_space=pltpu.VMEM)
    dma = pltpu.SemaphoreType.DMA
    modes = pl.pallas_call(
        functools.partial(kernel, (groups, spaces)),
        out_shape=jax.ShapeDtypeStruct((rank * cells // cells_z, cells_z), F32),
        in_specs=[pl.BlockSpec(memory_space=pltpu.HBM)] * 7,
        out_specs=vmem,
        scratch_shapes=[
            pltpu.VMEM(velocity.shape, BF16),
            pltpu.VMEM(block_id.shape, jnp.int32),
            pltpu.SMEM(metric.shape[::-1], F32),
            pltpu.VMEM(leaf_rot.shape, F32),
            pltpu.VMEM((merge_rot.shape[0], rank, 2 * rank), F32),
            pltpu.SMEM(merge_order.shape, jnp.int32),
            pltpu.SMEM(ref_cell.shape, jnp.int32),
            pltpu.VMEM((here * 3 * rows_y * cells_x, cells_z), F32),
            pltpu.VMEM((cells_x, tile_rows, cells_z), BF16),
            pltpu.VMEM((2, cells_x + 2, tile_rows, cells_z), BF16),
            pltpu.VMEM((groups, width_x, tile_rows, cells_z), BF16),
            pltpu.VMEM((groups, 2, width_x + 2, tile_rows, cells_z), BF16),
            pltpu.VMEM((2, groups, width_x, 2 * here, cells_z), BF16),
            pltpu.VMEM((2, groups, width_x, 2 * here, cells_z), BF16),
            pltpu.VMEM((groups, here, lead_width), F32),
            pltpu.VMEM((3, rows_y, width_x, cells_z), F32),
            pltpu.VMEM((total + gram_width, cells), BF16),
            pltpu.VMEM((spaces, share, gram_width), F32),
            pltpu.VMEM((spaces, share, gram_width), F32),
            pltpu.VMEM((groups, share, gram_width), F32),
            pltpu.VMEM((spaces, share, gram_width), F32),
        ]
        + [dma((7,))]
        + [dma((groups,))] * 6
        + [dma((2, groups))] * 2
        + [dma((spaces,))] * 2
        + [dma((groups,))] * 2
        + [dma((spaces,))] * 2,
        compiler_params=pltpu.CompilerParams(
            collective_id=0, has_side_effects=True, vmem_limit_bytes=56 * 1024 * 1024
        ),
    )(velocity, block_id, metric.T, leaf_rot, jnp.swapaxes(merge_rot, 1, 2), merge_order, ref_cell)
    modes = modes.reshape(rank, 3, width_x, rows_y, cells_z)
    return jnp.swapaxes(modes, 2, 3).reshape(rank, 3, rows_y, width_x * cells_z)


def solution(mesh):
    placed = (
        P("snap", None, "space", None, None),
        P("space", None, None),
        P(),
        P("snap", None, None),
        P(),
        P(),
        P(),
    )
    return jax.shard_map(
        local, mesh=mesh, in_specs=placed, out_specs=P(None, None, "space", "snap"), check_vma=False
    )
```
